512 devices in a mesh: fsdp: 16 (over x, z_hi, core), frame: 32 (over y, z_lo).
Axes of the slice: x: 4, y: 4, z: 16 (z_hi: 2, z_lo: 8; z = z_hi * 8 + z_lo), core: 2. Of those that a mesh axis runs over, the one named last changes fastest.
Arguments:
- temporal_out: bfloat16 [32768, 4096], P('frame', 'fsdp'), may hold values from -6 to 6
- norm_gain: bfloat16 [4096], P('fsdp'), may hold values from 0.25 to 1.75
- input_proj: bfloat16 [4096, 1024], P('fsdp'), may hold values from -0.09375 to 0.09375
- code_table: bfloat16 [1024, 1024], P('fsdp'), may hold values from -6 to 6
- depth_gain: bfloat16 [1024], replicated, may hold values from 0.25 to 1.75
- depth_proj: bfloat16 [1024, 3072], P('frame'), may hold values from -0.1875 to 0.1875
- depth_out: bfloat16 [1024, 1024], replicated, may hold values from -0.1875 to 0.1875
- code_ids: int32 [32, 16, 64, 8], P('frame', 'fsdp'), may hold values from 0 to 1023
Outputs:
- depth_stream: bfloat16 [32, 16, 64, 8, 1024], P('frame', 'fsdp')
The draws below stay inside these ranges and needn't reach their ends.
All inputs are finite; a program needn't handle non-finite values.
Results may differ from the reference program's by a relative error of at most 0.014.
Values may be sent and summed in bfloat16 or wider, within the bound.
A program may use at most 64 MiB of HBM per device.

```python
import jax
import jax.numpy as jnp
from jax import lax

D = 4096
E = 1024
HEADS = 16
HEAD = 64
CODEBOOKS = 8
VOCAB = 1024
FR_DEV = 64
TBLK = 1024
NBLK = 32
NSUB = 16
FRAMES = 32768


def set_ends(entries, own_key, least, top_value):
    longest = entries.shape.index(max(entries.shape))
    spots = []
    for shift in (0, 1):
        where = [jax.random.randint(jax.random.fold_in(own_key, axis), (), 0, length) for axis, length in enumerate(entries.shape)]
        where[longest] = (where[longest] + shift) % entries.shape[longest]
        spots.append(tuple(where))
    return entries.at[spots[0]].set(least).at[spots[1]].set(top_value)


def steps_of(rng, dims, split, low, top_value):
    def one(dim, blocks):
        heights = jax.random.uniform(jax.random.fold_in(jax.random.fold_in(rng, 6), dim), (blocks,), jnp.float32, low / len(split), top_value / len(split))
        return jnp.repeat(jnp.exp(heights), dims[dim] // blocks).reshape((-1,) + (1,) * (len(dims) - dim - 1))

    level = one(*split[0])
    for cut in split[1:]:
        level = level * one(*cut)
    return level


def scatter_about(own_key, extent, deviation, reach, pieces=(), dtype=jnp.bfloat16):
    entries = jax.random.normal(own_key, extent, jnp.float32) * deviation
    if len(pieces) > 0:
        entries = steps_of(own_key, extent, pieces, -0.22, 0.18) * entries
    return jnp.clip(entries, min=-reach, max=reach).astype(dtype)


def setup_inputs(seed: int = 0) -> dict:
    seeds = jax.random.split(jax.random.key(seed), 9)
    return {
        "temporal_out": scatter_about(seeds[0], (FRAMES, D), 1.0, 6.0, ((0, 32), (1, 16))),
        "norm_gain": jnp.clip(1.0 + 0.15 * jax.random.normal(seeds[1], (D,), jnp.float32), 0.25, 1.75).astype(jnp.bfloat16),
        "input_proj": scatter_about(seeds[2], (D, E), D ** -0.5, 0.09375, ((0, 16),)),
        "code_table": scatter_about(seeds[3], (VOCAB, E), 1.0, 6.0, ((0, 16),)),
        "depth_gain": jnp.clip(1.0 + 0.15 * jax.random.normal(seeds[4], (E,), jnp.float32), 0.25, 1.75).astype(jnp.bfloat16),
        "depth_proj": scatter_about(seeds[5], (E, 3 * E), E ** -0.5, 0.1875, ((0, 32),)),
        "depth_out": scatter_about(seeds[6], (E, E), E ** -0.5, 0.1875),
        "code_ids": set_ends(jax.random.randint(seeds[7], (NBLK, NSUB, FR_DEV, CODEBOOKS), 0, VOCAB), jax.random.fold_in(seeds[7], 1), 0, VOCAB - 1).astype(jnp.int32),
    }


def depth_block(context, codes, code_table, depth_gain, depth_proj, depth_out):
    embedded = jnp.take(code_table, codes, axis=0).astype(jnp.float32)
    stream = context.astype(jnp.float32)[:, None, :] + embedded
    inv_depth = lax.rsqrt(lax.optimization_barrier(jnp.mean(stream * stream, axis=-1, keepdims=True)) + 1e-05)
    normed = (stream * inv_depth * depth_gain.astype(jnp.float32)).astype(jnp.bfloat16)
    frames = stream.shape[0]
    qkv = jnp.dot(normed.reshape(-1, E), depth_proj, preferred_element_type=jnp.float32).astype(jnp.bfloat16)
    qkv = qkv.reshape(frames, CODEBOOKS, 3, HEADS, HEAD)
    queries = qkv[:, :, 0].astype(jnp.float32)
    keys = qkv[:, :, 1].astype(jnp.float32)
    values = qkv[:, :, 2].astype(jnp.float32)
    scores = jnp.einsum('fqhd,fkhd->fhqk', queries, keys) / jnp.sqrt(jnp.float32(HEAD))
    causal = jnp.arange(CODEBOOKS)[:, None] >= jnp.arange(CODEBOOKS)[None, :]
    scores = jnp.where(causal, scores, jnp.float32(-1e+30))
    weights = jax.nn.softmax(scores, axis=-1).astype(jnp.bfloat16)
    mixed = jnp.einsum('fhqk,fkhd->fqhd', weights.astype(jnp.float32), values).astype(jnp.bfloat16)
    update = jnp.dot(mixed.reshape(-1, E), depth_out, preferred_element_type=jnp.float32)
    return (stream.reshape(-1, E) + update).astype(jnp.bfloat16).reshape(frames, CODEBOOKS, E)

def reference(temporal_out, norm_gain, input_proj, code_table, depth_gain, depth_proj, depth_out, code_ids):
    blocks = temporal_out.reshape(NBLK, TBLK, D)

    def one_block(inputs):
        block, codes = inputs
        wide = block.astype(jnp.float32)
        inv_rms = lax.rsqrt(lax.optimization_barrier(jnp.mean(wide * wide, axis=1)) + 1e-05)
        scaled = (wide * norm_gain.astype(jnp.float32)).astype(jnp.bfloat16)
        context = (jnp.dot(scaled, input_proj, preferred_element_type=jnp.float32) * inv_rms[:, None]).astype(jnp.bfloat16)
        result = depth_block(context, codes.reshape(TBLK, CODEBOOKS), code_table, depth_gain, depth_proj, depth_out)
        return result.reshape(NSUB, FR_DEV, CODEBOOKS, E)
    return lax.map(one_block, (blocks, code_ids))
```

```python
import functools

import jax
import jax.numpy as jnp
from jax import lax
from jax.experimental import pallas as pl
from jax.experimental.pallas import tpu as pltpu
from jax.sharding import PartitionSpec as P

BF = jnp.bfloat16
F32 = jnp.float32
MESH = pl.DeviceIdType.MESH
NT = (((1,), (1,)), ((), ()))
N_REMOTE = 112


def dot(a, b):
    return jnp.dot(a, b, preferred_element_type=F32)


def kernel(
    temporal, gain, proj, table, dgain, dproj, dout, codes,
    out,
    tbuf, pbuf, gbuf, pacc, part, rel, rx, stg, zs, zr, zf,
    ssp, ssr, ssx, ssz,
    tab, emb, normed, stream,
    wb, qkv, mixed, doutb, outb,
    ssem, rsem, lsem,
):
    fs = lax.axis_index("fsdp")
    fr = lax.axis_index("frame")
    x, zh, c = fs // 4, lax.rem(fs // 2, 2), lax.rem(fs, 2)
    y, zl = fr // 8, lax.rem(fr, 8)
    z = zh * 8 + zl
    sib = 1 - c

    def at(dx=0, dy=0, dz=0, core=None):
        tx, ty, tz = lax.rem(x + dx + 4, 4), lax.rem(y + dy + 4, 4), lax.rem(z + dz + 16, 16)
        tc = c if core is None else core
        return (tx * 4 + (tz // 8) * 2 + tc, ty * 8 + lax.rem(tz, 8))

    x1, x2, x3 = lax.rem(x + 1, 4), lax.rem(x + 2, 4), lax.rem(x + 3, 4)
    y1, y2, y3 = lax.rem(y + 1, 4), lax.rem(y + 2, 4), lax.rem(y + 3, 4)

    started = []

    def send(src, dst, dev):
        index = len(started)
        copy = pltpu.make_async_remote_copy(
            src_ref=src, dst_ref=dst, send_sem=ssem.at[index], recv_sem=rsem.at[index],
            device_id=dev, device_id_type=MESH,
        )
        copy.start()
        started.append(copy)
        return copy

    locals_ = []

    def load(src, dst):
        copy = pltpu.make_async_copy(src, dst, lsem.at[len(locals_)])
        copy.start()
        locals_.append(copy)
        return copy

    j = x * 2 + c
    w_mine = pl.ds(pl.multiple_of(fr * 32, 32), 32)
    l_w = [
        load(
            dproj.at[:, pl.ds(pl.multiple_of(part_ * 1024 + j * 128, 128), 128)],
            wb.at[j, w_mine, pl.ds(part_ * 128, 128)],
        )
        for part_ in range(3)
    ]
    l_t = load(temporal.at[:, :, c], tbuf.at[c])
    l_p = load(proj, pbuf.at[c])
    l_tab = load(table, tab.at[fs])
    l_out = load(dout, doutb)
    gbuf[c] = jnp.broadcast_to(gain[...].astype(F32), (8, 256))

    partners = [at(core=sib), at(dx=1), at(dx=-1), at(dx=2), at(dy=1), at(dy=-1), at(dz=8)]
    partners += [at(dz=k) for k in (1, -1, 2, -2, 3, -3, 4, -4)]
    barrier = pltpu.get_barrier_semaphore()
    for partner in partners:
        pl.semaphore_signal(barrier, inc=1, device_id=partner, device_id_type=MESH)
    pl.semaphore_wait(barrier, len(partners))

    s_t = send(temporal.at[:, :, sib], tbuf.at[c], at(core=sib))
    s_p = send(proj, pbuf.at[c], at(core=sib))
    s_g = send(gbuf.at[c], gbuf.at[c], at(core=sib))
    for copy in l_w:
        copy.wait()
    s_wz = [
        send(wb.at[j, w_mine], wb.at[j, w_mine], at(dz=k)) for k in (4, 3, -3, 2, -2, 1, -1)
    ]
    quarter = pl.ds(pl.multiple_of(y * 16, 16), 16)
    s_tz = send(table.at[quarter], tab.at[fs, quarter], at(dz=8))
    s_tp = send(table, tab.at[fs], at(dx=1))
    s_tm = send(table, tab.at[fs], at(dx=-1))
    s_ts = send(table, tab.at[fs], at(core=sib))

    l_t.wait()
    l_p.wait()

    def scaled(k, half):
        rows = tbuf[k, :, half].reshape(256, 256).astype(F32)
        return (rows * gbuf[k][0:1]).astype(BF)

    far, near = 1 - zh, zh
    for side, half in ((0, far), (1, near)):
        pacc[side] = dot(scaled(c, half), pbuf[c])

    ids = codes[...]
    row = lax.broadcasted_iota(jnp.int32, (512, 64), 0)
    col = lax.broadcasted_iota(jnp.int32, (512, 64), 1)
    spread = (row // 8 == col).astype(BF)
    high = dot(spread, (ids // 32).astype(F32).astype(BF))
    low = dot(spread, lax.rem(ids, 32).astype(F32).astype(BF))
    row8 = lax.broadcasted_iota(jnp.int32, (512, 8), 0)
    col8 = lax.broadcasted_iota(jnp.int32, (512, 8), 1)
    picked = jnp.where(lax.rem(row8, 8) == col8, high * 32.0 + low, 0.0)
    id_col = jnp.sum(picked, axis=1, keepdims=True).astype(jnp.int32)

    s_t.wait_recv()
    s_p.wait_recv()
    s_g.wait_recv()
    s_x = []
    for side, half in ((0, far), (1, near)):
        total = pacc[side] + dot(scaled(sib, half), pbuf[sib])
        part[side] = total.astype(BF).reshape(4, 64, 1024)
        s_x.append((
            send(part.at[side, x2, 0:32], rel.at[side, 0], at(dx=1)),
            send(part.at[side, x2, 32:64], rel.at[side, 1], at(dx=-1)),
            send(part.at[side, x1, 32:64], rx.at[side, 0, 32:64], at(dx=1)),
            send(part.at[side, x3, 0:32], rx.at[side, 1, 0:32], at(dx=-1)),
        ))

    ones = jnp.ones((8, 256), BF)
    squares = jnp.zeros((8, 512), F32)
    for k in range(2):
        rows = tbuf[k].reshape(512, 256).astype(F32)
        sq = rows * rows
        hi = sq.astype(BF)
        lo = (sq - hi.astype(F32)).astype(BF)
        squares += lax.dot_general(ones, hi, NT, preferred_element_type=F32)
        squares += lax.dot_general(ones, lo, NT, preferred_element_type=F32)
    for k in range(4):
        ssp[k] = squares[:, 128 * k : 128 * (k + 1)]
    s_ss = [
        send(ssp.at[x1], ssr.at[0], at(dx=1)),
        send(ssp.at[x3], ssr.at[1], at(dx=-1)),
        send(ssp.at[x2], ssr.at[2], at(dx=2)),
    ]

    pieces = [lax.rem(x + k, 4) * 2 + c for k in (0, 3, 1, 2)]
    sib_pieces = [lax.rem(x + k, 4) * 2 + sib for k in (0, 3, 1, 2)]

    def block(yy):
        return pl.ds(pl.multiple_of(yy * 256, 256), 256)

    def half_block(yy, k):
        return pl.ds(pl.multiple_of(yy * 256 + 128 * k, 128), 128)

    s_wy, s_ws = {}, {}

    def spread_piece(r):
        p = pieces[r]
        s_wy[r] = [
            send(wb.at[p, block(y)], wb.at[p, block(y)], at(dy=1)),
            send(wb.at[p, block(y)], wb.at[p, block(y)], at(dy=-1)),
        ]
        s_ws[r] = [send(wb.at[p, block(y)], wb.at[p, block(y)], at(core=sib))]

    def relay_piece(r):
        p = pieces[r]
        s_wy[r][0].wait_recv()
        s_wy[r].append(send(wb.at[p, half_block(y3, 0)], wb.at[p, half_block(y3, 0)], at(dy=1)))
        s_ws[r].append(send(wb.at[p, block(y3)], wb.at[p, block(y3)], at(core=sib)))
        s_wy[r][1].wait_recv()
        s_wy[r].append(send(wb.at[p, half_block(y1, 1)], wb.at[p, half_block(y1, 1)], at(dy=-1)))
        s_ws[r].append(send(wb.at[p, block(y1)], wb.at[p, block(y1)], at(core=sib)))

    def finish_piece(r):
        p = pieces[r]
        s_wy[r][2].wait_recv()
        s_wy[r][3].wait_recv()
        s_ws[r].append(send(wb.at[p, block(y2)], wb.at[p, block(y2)], at(core=sib)))

    for copy in s_wz:
        copy.wait_recv()
    s_wx = [
        send(wb.at[j, block(y)], wb.at[j, block(y)], at(dx=1)),
        send(wb.at[j, block(y)], wb.at[j, block(y)], at(dx=-1)),
    ]
    spread_piece(0)

    def second_hop(side):
        s_x[side][0].wait_recv()
        stg[side, 0] = (part[side, x1, 0:32].astype(F32) + rel[side, 0].astype(F32)).astype(BF)
        a = send(stg.at[side, 0], rx.at[side, 0, 0:32], at(dx=1))
        s_x[side][1].wait_recv()
        stg[side, 1] = (part[side, x3, 32:64].astype(F32) + rel[side, 1].astype(F32)).astype(BF)
        b = send(stg.at[side, 1], rx.at[side, 1, 32:64], at(dx=-1))
        return a, b

    def x_total(side, hops):
        for copy in s_x[side][2:] + hops:
            copy.wait_recv()
        total = part[side, x].astype(F32) + rx[side, 0].astype(F32)
        return total + rx[side, 1].astype(F32)

    hops_far = second_hop(0)
    fz = x * 4 + (1 - zh) * 2 + c
    s_tz.wait_recv()
    s_ty = [
        send(tab.at[fz, quarter], tab.at[fz, quarter], at(dy=1)),
        send(tab.at[fz, quarter], tab.at[fz, quarter], at(dy=-1)),
    ]
    hops_near = second_hop(1)

    zs[...] = x_total(0, hops_far).astype(BF)
    s_z = [
        send(zs.at[0:32], zr.at[0], at(dz=4)),
        send(zs.at[32:64], zr.at[1], at(dz=-4)),
    ]
    for copy in s_ss:
        copy.wait_recv()
    ssx[...] = ssp[x] + ssr[0] + ssr[1] + ssr[2]
    s_ssz = send(ssx, ssz, at(dz=8))

    s_ty[0].wait_recv()
    q3 = pl.ds(pl.multiple_of(y3 * 16, 16), 16)
    s_ty.append(send(tab.at[fz, q3], tab.at[fz, q3], at(dy=1)))
    s_ty[1].wait_recv()

    def relay_x():
        p = pieces[1]
        s_wx[0].wait_recv()
        s_wx.append(send(wb.at[p, half_block(y, 0)], wb.at[p, half_block(y, 0)], at(dx=1)))
        spread_piece(1)
        p = pieces[2]
        s_wx[1].wait_recv()
        s_wx.append(send(wb.at[p, half_block(y, 1)], wb.at[p, half_block(y, 1)], at(dx=-1)))
        spread_piece(2)

    relay_x()
    f3, f1 = x3 * 4 + zh * 2 + c, x1 * 4 + zh * 2 + c
    s_tp.wait_recv()
    s_tm.wait_recv()
    s_tx = [
        send(tab.at[f3, 0:32], tab.at[f3, 0:32], at(dx=1)),
        send(tab.at[f1, 32:64], tab.at[f1, 32:64], at(dx=-1)),
        send(tab.at[f3], tab.at[f3], at(core=sib)),
        send(tab.at[f1], tab.at[f1], at(core=sib)),
    ]
    s_ty[2].wait_recv()
    s_uz = [
        send(tab.at[fz], tab.at[fz], at(dx=1)),
        send(tab.at[fz], tab.at[fz], at(dx=-1)),
        send(tab.at[fz], tab.at[fz], at(core=sib)),
    ]
    relay_piece(0)

    s_z[0].wait_recv()
    s_zz = [send(zr.at[0], zf.at[0:32], at(dz=4))]
    s_z[1].wait_recv()
    s_zz.append(send(zr.at[1], zf.at[32:64], at(dz=-4)))

    s_wx[2].wait_recv()
    s_wx[3].wait_recv()
    spread_piece(3)
    finish_piece(0)

    f2 = x2 * 4 + zh * 2 + c
    s_tx[0].wait_recv()
    s_tx[1].wait_recv()
    s_tx.append(send(tab.at[f2], tab.at[f2], at(core=sib)))
    g3, g1 = x3 * 4 + (1 - zh) * 2 + c, x1 * 4 + (1 - zh) * 2 + c
    s_uz[0].wait_recv()
    s_uz[1].wait_recv()
    s_ux = [
        send(tab.at[g3, 0:32], tab.at[g3, 0:32], at(dx=1)),
        send(tab.at[g1, 32:64], tab.at[g1, 32:64], at(dx=-1)),
        send(tab.at[g3], tab.at[g3], at(core=sib)),
        send(tab.at[g1], tab.at[g1], at(core=sib)),
    ]
    relay_piece(1)
    s_ux[0].wait_recv()
    s_ux[1].wait_recv()
    g2 = x2 * 4 + (1 - zh) * 2 + c
    s_ux.append(send(tab.at[g2], tab.at[g2], at(core=sib)))
    l_tab.wait()
    for copy in [s_ts, s_tx[2], s_tx[3], s_tx[4], s_uz[2], s_ux[2], s_ux[3], s_ux[4]]:
        copy.wait_recv()

    lanes = lax.broadcasted_iota(jnp.int32, (128, 1024), 1)
    whole_table = tab[...].reshape(1024, 1024)
    for t in range(4):
        onehot = (lanes == id_col[128 * t : 128 * (t + 1)]).astype(F32).astype(BF)
        emb[128 * t : 128 * (t + 1)] = dot(onehot, whole_table).astype(BF)
    finish_piece(1)
    relay_piece(2)

    near_total = x_total(1, hops_near)
    s_ssz.wait_recv()
    sums = ssx[...] + ssz[...]
    for copy in s_zz:
        copy.wait_recv()
    lane = lax.broadcasted_iota(jnp.int32, (64, 128), 1)
    sub = lax.broadcasted_iota(jnp.int32, (64, 128), 0)
    sum_col = jnp.sum(
        jnp.where(lane == sub + 64 * zh, sums[0:1], 0.0), axis=1, keepdims=True
    )
    inv_rms = lax.rsqrt(sum_col * (1.0 / 4096.0) + 1e-05)
    context = ((near_total + zf[...].astype(F32)) * inv_rms).astype(BF).astype(F32)
    depth_gain = dgain[...].astype(F32)
    for t in range(4):
        rows = slice(128 * t, 128 * (t + 1))
        wide = jnp.broadcast_to(context[16 * t : 16 * (t + 1)][:, None, :], (16, 8, 1024))
        value = wide.reshape(128, 1024) + emb[rows].astype(F32)
        inv = lax.rsqrt(jnp.mean(value * value, axis=-1, keepdims=True) + 1e-05)
        stream[rows] = value
        normed[rows] = (value * inv * depth_gain).astype(BF)
    finish_piece(2)
    relay_piece(3)

    first = lax.broadcasted_iota(jnp.int32, (128, 128), 1) < 64
    tr = lax.broadcasted_iota(jnp.int32, (128, 128), 0)
    tc = lax.broadcasted_iota(jnp.int32, (128, 128), 1)
    allowed = (tr // 8 == tc // 8) & (tc <= tr)

    def attend(p, slot):
        qkv[...] = dot(normed[...], wb[p]).astype(BF)

        def tile(t, carry):
            rows = pl.ds(pl.multiple_of(t * 128, 128), 128)
            q = qkv[rows, 0:128].astype(F32) * 0.125
            k = qkv[rows, 128:256]
            v = qkv[rows, 256:384]
            results = []
            for head in range(2):
                keep = first if head == 0 else jnp.logical_not(first)
                qh = jnp.where(keep, q, 0.0).astype(BF)
                scores = lax.dot_general(qh, k, NT, preferred_element_type=F32)
                scores = jnp.where(allowed, scores, -1e30)
                top = jnp.max(scores, axis=1, keepdims=True)
                e = jnp.exp(scores - top)
                weights = (e / jnp.sum(e, axis=1, keepdims=True)).astype(BF)
                results.append(dot(weights, v))
            mixed[rows, pl.ds(pl.multiple_of(slot * 128, 128), 128)] = jnp.where(
                first, results[0], results[1]
            ).astype(BF)
            return carry

        lax.fori_loop(0, 4, tile, 0)

    for r in range(4):
        if r == 3:
            finish_piece(3)
        attend(pieces[r], c)
        for copy in s_ws[r]:
            copy.wait_recv()
        attend(sib_pieces[r], sib)
        if r == 0:
            l_out.wait()
        weights_out = doutb[
            pl.ds(pl.multiple_of(lax.rem(x + (0, 3, 1, 2)[r], 4) * 256, 256), 256)
        ]
        if r < 3:
            stream[...] = stream[...] + dot(mixed[...], weights_out)
        else:
            stores = []
            for t in range(4):
                rows = slice(128 * t, 128 * (t + 1))
                outb[rows] = (stream[rows] + dot(mixed[rows], weights_out)).astype(BF)
                stores.append(load(outb.at[rows], out.at[rows]))
            for copy in stores:
                copy.wait()

    for copy in started:
        copy.wait_send()


def per_device(
    temporal_out, norm_gain, input_proj, code_table, depth_gain, depth_proj, depth_out, code_ids
):
    vmem = pl.BlockSpec(memory_space=pltpu.VMEM)
    hbm = pl.BlockSpec(memory_space=pl.ANY)
    scratch = [
        ((2, 4, 2, 64, 256), BF),
        ((2, 256, 1024), BF),
        ((2, 8, 256), F32),
        ((2, 256, 1024), F32),
        ((2, 4, 64, 1024), BF),
        ((2, 2, 32, 1024), BF),
        ((2, 2, 64, 1024), BF),
        ((2, 2, 32, 1024), BF),
        ((64, 1024), BF),
        ((2, 32, 1024), BF),
        ((64, 1024), BF),
        ((4, 8, 128), F32),
        ((3, 8, 128), F32),
        ((8, 128), F32),
        ((8, 128), F32),
        ((16, 64, 1024), BF),
        ((512, 1024), BF),
        ((512, 1024), BF),
        ((512, 1024), F32),
        ((8, 1024, 384), BF),
        ((512, 384), BF),
        ((512, 256), BF),
        ((1024, 1024), BF),
        ((512, 1024), BF),
    ]
    result = pl.pallas_call(
        kernel,
        out_shape=jax.ShapeDtypeStruct((512, 1024), BF),
        in_specs=[hbm, vmem, hbm, hbm, vmem, hbm, hbm, vmem],
        out_specs=hbm,
        scratch_shapes=[pltpu.VMEM(shape, dtype) for shape, dtype in scratch]
        + [
            pltpu.SemaphoreType.DMA((N_REMOTE,)),
            pltpu.SemaphoreType.DMA((N_REMOTE,)),
            pltpu.SemaphoreType.DMA((16,)),
        ],
        compiler_params=pltpu.CompilerParams(
            collective_id=0, has_side_effects=True, vmem_limit_bytes=56 * 1024 * 1024
        ),
        cost_estimate=pl.CostEstimate(
            flops=6_500_000_000, bytes_accessed=6_000_000, transcendentals=2_000_000
        ),
    )(
        temporal_out.reshape(4, 2, 2, 64, 256),
        norm_gain.reshape(1, 256),
        input_proj,
        code_table,
        depth_gain.reshape(1, 1024),
        depth_proj,
        depth_out,
        code_ids.reshape(64, 8),
    )
    return result.reshape(1, 1, 64, 8, 1024)


def solution(mesh):
    placed = (
        P("frame", "fsdp"),
        P("fsdp"),
        P("fsdp", None),
        P("fsdp", None),
        P(),
        P("frame", None),
        P(),
        P("frame", "fsdp", None, None),
    )
    return jax.shard_map(
        per_device,
        mesh=mesh,
        in_specs=placed,
        out_specs=P("frame", "fsdp", None, None, None),
        check_vma=False,
    )
```

```python
import functools

import jax
import jax.numpy as jnp
from jax import lax
from jax.experimental import pallas as pl
from jax.experimental.pallas import tpu as pltpu
from jax.sharding import PartitionSpec as P

BF = jnp.bfloat16
F32 = jnp.float32
MESH = pl.DeviceIdType.MESH
NT = (((1,), (1,)), ((), ()))
N_REMOTE = 128


def dot(a, b):
    return jnp.dot(a, b, preferred_element_type=F32)


def kernel(
    temporal, gain, proj, table, dgain, dproj, dout, codes,
    out,
    tbuf, pbuf, gbuf, pacc, part, rel, rx, stg, fx, zs, zf,
    ssp, ssr, ssx, ssz,
    tab, emb, normed, stream,
    wb, qkv, comp, expand, mixed, doutb, outb,
    ssem, rsem, lsem,
):
    fs = lax.axis_index("fsdp")
    fr = lax.axis_index("frame")
    x, zh, c = fs // 4, lax.rem(fs // 2, 2), lax.rem(fs, 2)
    y, zl = fr // 8, lax.rem(fr, 8)
    z = zh * 8 + zl
    sib = 1 - c

    def at(dx=0, dy=0, dz=0, core=None):
        tx, ty, tz = lax.rem(x + dx + 4, 4), lax.rem(y + dy + 4, 4), lax.rem(z + dz + 16, 16)
        tc = c if core is None else core
        return (tx * 4 + (tz // 8) * 2 + tc, ty * 8 + lax.rem(tz, 8))

    x1, x2, x3 = lax.rem(x + 1, 4), lax.rem(x + 2, 4), lax.rem(x + 3, 4)
    y1, y2, y3 = lax.rem(y + 1, 4), lax.rem(y + 2, 4), lax.rem(y + 3, 4)

    started = []

    def send(src, dst, dev):
        index = len(started)
        copy = pltpu.make_async_remote_copy(
            src_ref=src, dst_ref=dst, send_sem=ssem.at[index], recv_sem=rsem.at[index],
            device_id=dev, device_id_type=MESH,
        )
        copy.start()
        started.append(copy)
        return copy

    locals_ = []

    def load(src, dst):
        copy = pltpu.make_async_copy(src, dst, lsem.at[len(locals_)])
        copy.start()
        locals_.append(copy)
        return copy

    mine = pl.ds(pl.multiple_of(c * 384, 128), 384)
    ring = [lax.rem(x + k, 4) for k in (0, 3, 1, 2)]

    def near_rows(yy, place):
        return pl.ds(pl.multiple_of(yy * 256 + 32 * place, 32), 32)

    def far_rows(yy):
        return pl.ds(pl.multiple_of(yy * 256 + 64, 32), 160)

    def far_half(yy, k):
        return pl.ds(pl.multiple_of(yy * 256 + 64 + 80 * k, 16), 80)

    l_w = [
        load(
            dproj.at[:, pl.ds(pl.multiple_of(k * 1024 + (2 * xx + c) * 128, 128), 128)],
            wb.at[xx, near_rows(y, 0), pl.ds(pl.multiple_of(c * 384 + k * 128, 128), 128)],
        )
        for xx in range(4)
        for k in range(3)
    ]
    l_t = load(temporal.at[:, :, c], tbuf.at[c])
    l_p = load(proj, pbuf.at[c])
    l_tab = load(table, tab.at[fs])
    l_out = load(dout, doutb)
    gbuf[c] = jnp.broadcast_to(gain[...].astype(F32).reshape(1, 256), (8, 256))

    partners = [at(core=sib), at(dx=1), at(dx=-1), at(dx=2), at(dy=1), at(dy=-1), at(dy=2)]
    partners += [at(dz=k) for k in (1, -1, 2, -2, 3, -3, 4, -4, 8)]
    barrier = pltpu.get_barrier_semaphore()
    for partner in partners:
        pl.semaphore_signal(barrier, inc=1, device_id=partner, device_id_type=MESH)
    pl.semaphore_wait(barrier, len(partners))

    s_t = send(temporal.at[:, :, sib], tbuf.at[c], at(core=sib))
    s_p = send(proj, pbuf.at[c], at(core=sib))
    s_g = send(gbuf.at[c], gbuf.at[c], at(core=sib))
    for copy in l_w:
        copy.wait()

    def send_w(xx, rows, **to):
        ref = wb.at[xx, rows, mine]
        return send(ref, ref, at(**to))

    s_wz = [
        send(wb.at[x, near_rows(y, 0), mine], wb.at[x, near_rows(y, -k % 8), mine], at(dz=k))
        for k in (4, 3, -3, 2, -2)
    ]
    s_wn = [
        send(wb.at[:, near_rows(y, 0), mine], wb.at[:, near_rows(y, -k % 8), mine], at(dz=k))
        for k in (1, -1)
    ]
    every = slice(0, 4)
    up = {0: send_w(every, near_rows(y, 0), dy=1)}
    down = {0: send_w(every, near_rows(y, 0), dy=-1)}
    quarter = pl.ds(pl.multiple_of(y * 16, 16), 16)
    s_tz = send(table.at[quarter], tab.at[fs, quarter], at(dz=8))
    s_tp = send(table, tab.at[fs], at(dx=1))
    s_tm = send(table, tab.at[fs], at(dx=-1))
    s_ts = send(table, tab.at[fs], at(core=sib))

    l_t.wait()
    l_p.wait()

    def scaled(k, half):
        rows = tbuf[k, :, half].reshape(256, 256).astype(F32)
        return (rows * gbuf[k][0:1]).astype(BF)

    far, near = 1 - zh, zh
    for side, half in ((0, far), (1, near)):
        pacc[side] = dot(scaled(c, half), pbuf[c])
    s_t.wait_recv()
    s_p.wait_recv()
    s_g.wait_recv()

    def partial(side, half):
        total = pacc[side] + dot(scaled(sib, half), pbuf[sib])
        part[side] = total.astype(BF).reshape(4, 64, 1024)

    partial(0, far)
    s_f = []
    for k in range(2):
        rows = slice(32 * k, 32 * k + 32)
        s_f.append([
            send(part.at[0, x2, rows], fx.at[2, rows], at(dx=2)),
            send(part.at[0, x1, rows], fx.at[0, rows], at(dx=1)),
            send(part.at[0, x3, rows], fx.at[1, rows], at(dx=-1)),
        ])
    partial(1, near)

    def first_hop():
        return (
            send(part.at[1, x2, 0:32], rel.at[0], at(dx=1)),
            send(part.at[1, x2, 32:64], rel.at[1], at(dx=-1)),
            send(part.at[1, x1, 32:64], rx.at[0, 32:64], at(dx=1)),
            send(part.at[1, x3, 0:32], rx.at[1, 0:32], at(dx=-1)),
        )

    def second_hop():
        s_x[0].wait_recv()
        stg[0] = (part[1, x1, 0:32].astype(F32) + rel[0].astype(F32)).astype(BF)
        a = send(stg.at[0], rx.at[0, 0:32], at(dx=1))
        s_x[1].wait_recv()
        stg[1] = (part[1, x3, 32:64].astype(F32) + rel[1].astype(F32)).astype(BF)
        b = send(stg.at[1], rx.at[1, 32:64], at(dx=-1))
        return a, b

    def spread_near(place):
        up[place] = send_w(every, near_rows(y, place), dy=1)
        down[place] = send_w(every, near_rows(y, place), dy=-1)

    s_yn, s_sn = [], []

    def relay_near(place):
        up[place].wait_recv()
        s_yn.append(send_w(slice(0, 2), near_rows(y3, place), dy=1))
        down[place].wait_recv()
        s_yn.append(send_w(slice(2, 4), near_rows(y1, place), dy=-1))

    def share_near(yy):
        s_sn.append(send_w(every, pl.ds(pl.multiple_of(yy * 256, 256), 64), core=sib))
        s_sn.append(send_w(every, near_rows(yy, 7), core=sib))

    s_wn[0].wait_recv()
    spread_near(7)
    s_wn[1].wait_recv()
    spread_near(1)
    share_near(y)
    relay_near(0)

    s_wy, s_ws = {}, {}

    def spread_far(r):
        s_wy[r] = [send_w(ring[r], far_rows(y), dy=1), send_w(ring[r], far_rows(y), dy=-1)]
        s_ws[r] = [send_w(ring[r], far_rows(y), core=sib)]

    def relay_far(r):
        s_wy[r][0].wait_recv()
        s_wy[r].append(send_w(ring[r], far_half(y3, 0), dy=1))
        s_ws[r].append(send_w(ring[r], far_rows(y3), core=sib))
        s_wy[r][1].wait_recv()
        s_wy[r].append(send_w(ring[r], far_half(y1, 1), dy=-1))
        s_ws[r].append(send_w(ring[r], far_rows(y1), core=sib))

    def finish_far(r):
        for copy in s_wy[r][2:]:
            copy.wait_recv()
        s_ws[r].append(send_w(ring[r], far_rows(y2), core=sib))

    def across(k):
        rows = slice(32 * k, 32 * k + 32)
        for copy in s_f[k]:
            copy.wait_recv()
        total = part[0, x, rows].astype(F32) + fx[0, rows].astype(F32)
        total = total + fx[1, rows].astype(F32) + fx[2, rows].astype(F32)
        zs[rows] = total.astype(BF)
        return send(zs.at[rows], zf.at[rows], at(dz=8))

    s_z = [across(0)]
    for copy in s_wz:
        copy.wait_recv()
    s_wx = [send_w(x, far_rows(y), dx=1), send_w(x, far_rows(y), dx=-1)]
    spread_far(0)
    relay_near(7)
    relay_near(1)
    s_z.append(across(1))
    s_x = first_hop()

    ones = jnp.ones((8, 256), BF)
    squares = jnp.zeros((8, 512), F32)
    for k in range(2):
        rows = tbuf[k].reshape(512, 256).astype(F32)
        sq = rows * rows
        hi = sq.astype(BF)
        lo = (sq - hi.astype(F32)).astype(BF)
        squares += lax.dot_general(ones, hi, NT, preferred_element_type=F32)
        squares += lax.dot_general(ones, lo, NT, preferred_element_type=F32)
    for k in range(4):
        ssp[k] = squares[:, 128 * k : 128 * (k + 1)]
    s_ss = [
        send(ssp.at[x1], ssr.at[0], at(dx=1)),
        send(ssp.at[x3], ssr.at[1], at(dx=-1)),
        send(ssp.at[x2], ssr.at[2], at(dx=2)),
    ]

    ids = codes[...]
    row = lax.broadcasted_iota(jnp.int32, (512, 64), 0)
    col = lax.broadcasted_iota(jnp.int32, (512, 64), 1)
    spread = (row // 8 == col).astype(BF)
    high = (ids // 32).astype(F32).astype(BF)
    low = lax.rem(ids, 32).astype(F32).astype(BF)
    high = lax.dot_general(spread, high, NT, preferred_element_type=F32)
    low = lax.dot_general(spread, low, NT, preferred_element_type=F32)
    row8 = lax.broadcasted_iota(jnp.int32, (512, 8), 0)
    col8 = lax.broadcasted_iota(jnp.int32, (512, 8), 1)
    picked = jnp.where(lax.rem(row8, 8) == col8, high * 32.0 + low, 0.0)
    id_col = jnp.sum(picked, axis=1, keepdims=True).astype(jnp.int32)

    fz = x * 4 + (1 - zh) * 2 + c
    s_tz.wait_recv()
    s_ty = [send(tab.at[fz, quarter], tab.at[fz, quarter], at(dy=k)) for k in (1, -1, 2)]

    er = lax.broadcasted_iota(jnp.int32, (128, 256), 0)
    ec = lax.broadcasted_iota(jnp.int32, (128, 256), 1)
    for u in range(8):
        expand[u] = ((er // 8 == 2 * u + ec // 128) & (lax.rem(er, 8) == lax.rem(ec, 8))).astype(
            F32
        ).astype(BF)

    s_wx[0].wait_recv()
    s_wx.append(send_w(ring[1], far_half(y, 0), dx=1))
    spread_far(1)
    s_wx[1].wait_recv()
    s_wx.append(send_w(ring[2], far_half(y, 1), dx=-1))
    spread_far(2)
    relay_far(0)
    hops = second_hop()
    for copy in s_ss:
        copy.wait_recv()
    ssx[...] = ssp[x] + ssr[0] + ssr[1] + ssr[2]
    s_ssz = send(ssx, ssz, at(dz=8))

    f3, f1 = x3 * 4 + zh * 2 + c, x1 * 4 + zh * 2 + c
    s_tp.wait_recv()
    s_tm.wait_recv()
    s_tx = [
        send(tab.at[f3, 0:32], tab.at[f3, 0:32], at(dx=1)),
        send(tab.at[f1, 32:64], tab.at[f1, 32:64], at(dx=-1)),
        send(tab.at[f3], tab.at[f3], at(core=sib)),
        send(tab.at[f1], tab.at[f1], at(core=sib)),
    ]
    for copy in s_ty:
        copy.wait_recv()
    s_uz = [
        send(tab.at[fz], tab.at[fz], at(dx=1)),
        send(tab.at[fz], tab.at[fz], at(dx=-1)),
        send(tab.at[fz], tab.at[fz], at(core=sib)),
    ]
    s_wx[2].wait_recv()
    s_wx[3].wait_recv()
    spread_far(3)
    for copy in s_yn:
        copy.wait_recv()
    for yy in (y1, y2, y3):
        share_near(yy)
    finish_far(0)

    f2 = x2 * 4 + zh * 2 + c
    s_tx[0].wait_recv()
    s_tx[1].wait_recv()
    s_tx.append(send(tab.at[f2], tab.at[f2], at(core=sib)))
    g3, g1 = x3 * 4 + (1 - zh) * 2 + c, x1 * 4 + (1 - zh) * 2 + c
    s_uz[0].wait_recv()
    s_uz[1].wait_recv()
    s_ux = [
        send(tab.at[g3, 0:32], tab.at[g3, 0:32], at(dx=1)),
        send(tab.at[g1, 32:64], tab.at[g1, 32:64], at(dx=-1)),
        send(tab.at[g3], tab.at[g3], at(core=sib)),
        send(tab.at[g1], tab.at[g1], at(core=sib)),
    ]
    relay_far(1)
    s_ux[0].wait_recv()
    s_ux[1].wait_recv()
    g2 = x2 * 4 + (1 - zh) * 2 + c
    s_ux.append(send(tab.at[g2], tab.at[g2], at(core=sib)))
    l_tab.wait()
    for copy in [s_ts, s_tx[2], s_tx[3], s_tx[4], s_uz[2], s_ux[2], s_ux[3], s_ux[4]]:
        copy.wait_recv()

    lanes = lax.broadcasted_iota(jnp.int32, (128, 1024), 1)
    whole_table = tab[...].reshape(1024, 1024)
    for t in range(4):
        onehot = (lanes == id_col[128 * t : 128 * (t + 1)]).astype(F32).astype(BF)
        emb[128 * t : 128 * (t + 1)] = dot(onehot, whole_table).astype(BF)

    for copy in s_x[2:] + hops:
        copy.wait_recv()
    total = part[1, x].astype(F32) + rx[0].astype(F32) + rx[1].astype(F32)
    s_ssz.wait_recv()
    sums = ssx[...] + ssz[...]
    lane = lax.broadcasted_iota(jnp.int32, (64, 128), 1)
    sub = lax.broadcasted_iota(jnp.int32, (64, 128), 0)
    sum_col = jnp.sum(
        jnp.where(lane == sub + 64 * zh, sums[0:1], 0.0), axis=1, keepdims=True
    )
    inv_rms = lax.rsqrt(sum_col * (1.0 / 4096.0) + 1e-05)
    for copy in s_z:
        copy.wait_recv()
    context = ((total + zf[...].astype(F32)) * inv_rms).astype(BF).astype(F32)
    depth_gain = dgain[...].astype(F32).reshape(1, 1024)
    turn = lax.rem(256 - 32 * zl, 256)
    for t in range(4):
        rows = slice(128 * t, 128 * (t + 1))
        wide = jnp.broadcast_to(context[16 * t : 16 * (t + 1)][:, None, :], (16, 8, 1024))
        value = wide.reshape(128, 1024) + emb[rows].astype(F32)
        inv = lax.rsqrt(jnp.mean(value * value, axis=-1, keepdims=True) + 1e-05)
        stream[rows] = value
        value = value * inv * depth_gain
        for k in range(4):
            part_k = pltpu.roll(value[:, 256 * k : 256 * (k + 1)], turn, 1)
            normed[rows, 256 * k : 256 * (k + 1)] = part_k.astype(BF)
    relay_far(2)

    first = lax.broadcasted_iota(jnp.int32, (128, 128), 1) < 64
    frame_of_lane = lax.broadcasted_iota(jnp.int32, (8, 128), 1) // 8
    position = lax.broadcasted_iota(jnp.int32, (128, 128), 0)
    query = lax.broadcasted_iota(jnp.int32, (128, 128), 1)
    allowed = lax.rem(position, 8) <= lax.rem(query, 8)
    same_frame = (
        lax.broadcasted_iota(jnp.int32, (128, 256), 0) // 8
        == lax.rem(lax.broadcasted_iota(jnp.int32, (128, 256), 1), 128) // 8
    )

    def by_head(a):
        a = a.astype(F32)
        return jnp.concatenate(
            [jnp.where(first, a, 0.0).astype(BF), jnp.where(first, 0.0, a).astype(BF)], axis=0
        )

    def attend(xx):
        qkv[...] = dot(normed[...], wb[xx]).astype(BF)
        for t in range(4):
            rows = slice(128 * t, 128 * (t + 1))
            for b in range(2):
                q = qkv[rows, 384 * b : 384 * b + 128]
                k = by_head(qkv[rows, 384 * b + 128 : 384 * b + 256])
                scores = lax.dot_general(k, q, NT, preferred_element_type=F32)
                for h in range(2):
                    own = scores[128 * h : 128 * h + 8]
                    for f in range(1, 16):
                        own = jnp.where(
                            frame_of_lane == f, scores[128 * h + 8 * f : 128 * h + 8 * f + 8], own
                        )
                    unit = t * 4 + b * 2 + h
                    comp[8 * unit : 8 * unit + 8] = own
        scores = jnp.where(allowed, comp[...] * 0.125, -1e30).reshape(16, 8, 128)
        e = jnp.exp(scores - jnp.max(scores, axis=1, keepdims=True))
        weights = (e / jnp.sum(e, axis=1, keepdims=True)).reshape(128, 128)
        weights = weights.T.astype(BF)
        for t in range(4):
            rows = slice(128 * t, 128 * (t + 1))
            for b in range(2):
                wide = dot(weights, expand[t * 2 + b])
                wide = jnp.where(same_frame, wide, 0.0).astype(BF)
                v = by_head(qkv[rows, 384 * b + 256 : 384 * b + 384])
                mixed[rows, 128 * b : 128 * b + 128] = dot(wide, v).astype(BF)

    l_out.wait()
    for copy in s_sn:
        copy.wait_recv()
    for r in range(4):
        if r > 0:
            finish_far(r)
        if r == 1:
            relay_far(3)
        for copy in s_ws[r]:
            copy.wait_recv()
        attend(ring[r])
        weights_out = doutb[pl.ds(pl.multiple_of(ring[r] * 256, 256), 256)]
        if r < 3:
            stream[...] = stream[...] + dot(mixed[...], weights_out)
        else:
            stores = []
            for t in range(4):
                rows = slice(128 * t, 128 * (t + 1))
                outb[rows] = (stream[rows] + dot(mixed[rows], weights_out)).astype(BF)
                stores.append(load(outb.at[rows], out.at[rows]))
            for copy in stores:
                copy.wait()

    for copy in started:
        copy.wait_send()


def per_device(
    temporal_out, norm_gain, input_proj, code_table, depth_gain, depth_proj, depth_out, code_ids
):
    vmem = pl.BlockSpec(memory_space=pltpu.VMEM)
    hbm = pl.BlockSpec(memory_space=pl.ANY)
    scratch = [
        ((2, 4, 2, 64, 256), BF),
        ((2, 256, 1024), BF),
        ((2, 8, 256), F32),
        ((2, 256, 1024), F32),
        ((2, 4, 64, 1024), BF),
        ((2, 32, 1024), BF),
        ((2, 64, 1024), BF),
        ((2, 32, 1024), BF),
        ((3, 64, 1024), BF),
        ((64, 1024), BF),
        ((64, 1024), BF),
        ((4, 8, 128), F32),
        ((3, 8, 128), F32),
        ((8, 128), F32),
        ((8, 128), F32),
        ((16, 64, 1024), BF),
        ((512, 1024), BF),
        ((512, 1024), BF),
        ((512, 1024), F32),
        ((4, 1024, 768), BF),
        ((512, 768), BF),
        ((128, 128), F32),
        ((8, 128, 256), BF),
        ((512, 256), BF),
        ((1024, 1024), BF),
        ((512, 1024), BF),
    ]
    operands = (
        temporal_out.reshape(4, 2, 2, 64, 256),
        norm_gain,
        input_proj,
        code_table,
        depth_gain,
        depth_proj,
        depth_out,
        code_ids.reshape(64, 8).T,
    )
    result = pl.pallas_call(
        kernel,
        out_shape=jax.ShapeDtypeStruct((512, 1024), BF),
        in_specs=[hbm, vmem, hbm, hbm, vmem, hbm, hbm, vmem],
        out_specs=hbm,
        scratch_shapes=[pltpu.VMEM(shape, dtype) for shape, dtype in scratch]
        + [
            pltpu.SemaphoreType.DMA((N_REMOTE,)),
            pltpu.SemaphoreType.DMA((N_REMOTE,)),
            pltpu.SemaphoreType.DMA((24,)),
        ],
        compiler_params=pltpu.CompilerParams(
            collective_id=0, has_side_effects=True, vmem_limit_bytes=40 * 1024 * 1024
        ),
        cost_estimate=pl.CostEstimate(
            flops=6_500_000_000, bytes_accessed=6_000_000, transcendentals=2_000_000
        ),
    )(*(pltpu.with_memory_space_constraint(a, pltpu.HBM) for a in operands))
    return result.reshape(1, 1, 64, 8, 1024)


def solution(mesh):
    placed = (
        P("frame", "fsdp"),
        P("fsdp"),
        P("fsdp", None),
        P("fsdp", None),
        P(),
        P("frame", None),
        P(),
        P("frame", "fsdp", None, None),
    )
    return jax.shard_map(
        per_device,
        mesh=mesh,
        in_specs=placed,
        out_specs=P("frame", "fsdp", None, None, None),
        check_vma=False,
    )
```

```python
import functools

import jax
import jax.numpy as jnp
from jax import lax
from jax.experimental import pallas as pl
from jax.experimental.pallas import tpu as pltpu
from jax.sharding import PartitionSpec as P

BF = jnp.bfloat16
F32 = jnp.float32
MESH = pl.DeviceIdType.MESH
NT = (((1,), (1,)), ((), ()))
TN = (((0,), (0,)), ((), ()))
N_REMOTE = 128


def dot(a, b):
    return jnp.dot(a, b, preferred_element_type=F32)


def kernel(
    temporal, gain, proj, table, dgain, dproj, dout, codes,
    out,
    tbuf, pbuf, gbuf, pacc, part, rel, rx, stg, fx, zs, zf,
    ssp, ssr, ssx, ssz,
    tab, emb, normed, stream,
    wb, qkv, comp, mixed, doutb, outb,
    ssem, rsem, lsem,
):
    fs = lax.axis_index("fsdp")
    fr = lax.axis_index("frame")
    x, zh, c = fs // 4, lax.rem(fs // 2, 2), lax.rem(fs, 2)
    y, zl = fr // 8, lax.rem(fr, 8)
    z = zh * 8 + zl
    sib = 1 - c

    def at(dx=0, dy=0, dz=0, core=None):
        tx, ty, tz = lax.rem(x + dx + 4, 4), lax.rem(y + dy + 4, 4), lax.rem(z + dz + 16, 16)
        tc = c if core is None else core
        return (tx * 4 + (tz // 8) * 2 + tc, ty * 8 + lax.rem(tz, 8))

    x1, x2, x3 = lax.rem(x + 1, 4), lax.rem(x + 2, 4), lax.rem(x + 3, 4)
    y1, y2, y3 = lax.rem(y + 1, 4), lax.rem(y + 2, 4), lax.rem(y + 3, 4)

    started = []

    def send(src, dst, dev):
        index = len(started)
        copy = pltpu.make_async_remote_copy(
            src_ref=src, dst_ref=dst, send_sem=ssem.at[index], recv_sem=rsem.at[index],
            device_id=dev, device_id_type=MESH,
        )
        copy.start()
        started.append(copy)
        return copy

    locals_ = []

    def load(src, dst):
        copy = pltpu.make_async_copy(src, dst, lsem.at[len(locals_)])
        copy.start()
        locals_.append(copy)
        return copy

    mine = pl.ds(pl.multiple_of(c * 384, 128), 384)
    ring = [lax.rem(x + k, 4) for k in range(4)]

    def at_place(yy, place):
        return pl.ds(pl.multiple_of(yy * 256 + 32 * place, 32), 32)

    def far_rows(yy):
        return pl.ds(pl.multiple_of(yy * 256 + 96, 32), 96)

    def far_half(yy, k):
        return pl.ds(pl.multiple_of(yy * 256 + 96 + 48 * k, 16), 48)

    l_w = [
        load(
            dproj.at[:, pl.ds(pl.multiple_of(k * 1024 + (2 * xx + c) * 128, 128), 128)],
            wb.at[xx, at_place(y, 0), pl.ds(pl.multiple_of(c * 384 + k * 128, 128), 128)],
        )
        for xx in range(4)
        for k in range(3)
    ]
    l_t = load(temporal.at[:, :, c], tbuf.at[c])
    l_p = load(proj, pbuf.at[c])
    l_tab = load(table, tab.at[fs])
    l_out = [
        load(dout.at[pl.ds(pl.multiple_of(ring[r] * 256, 256), 256)], doutb.at[256 * r : 256 * r + 256])
        for r in range(4)
    ]
    gbuf[c] = jnp.broadcast_to(gain[...].astype(F32).reshape(1, 256), (8, 256))

    partners = [at(core=sib)]
    partners += [at(dx=k) for k in (1, -1, 2)] + [at(dy=k) for k in (1, -1, 2)]
    partners += [at(dz=k) for k in (1, -1, 8)]
    barrier = pltpu.get_barrier_semaphore()
    for partner in partners:
        pl.semaphore_signal(barrier, inc=1, device_id=partner, device_id_type=MESH)
    pl.semaphore_wait(barrier, len(partners))

    quarter = pl.ds(pl.multiple_of(y * 16, 16), 16)
    s_tz = send(table.at[quarter], tab.at[fs, quarter], at(dz=8))
    for copy in l_w:
        copy.wait()

    def send_w(xx, rows, **to):
        ref = wb.at[xx, rows, mine]
        return send(ref, ref, at(**to))

    every = slice(0, 4)

    def along_z(place, dz, pieces=slice(0, 4)):
        return send(
            wb.at[pieces, at_place(y, place), mine],
            wb.at[pieces, at_place(y, (place - dz) % 8), mine],
            at(dz=dz),
        )

    halves = (slice(0, 2), slice(2, 4))
    from_z = {}
    for k in range(2):
        for place, dz in ((7, 1), (1, -1)):
            from_z[place, k] = along_z(0, dz, halves[k])
    up = {0: send_w(every, at_place(y, 0), dy=1)}
    down = {0: send_w(every, at_place(y, 0), dy=-1)}
    s_t = send(temporal.at[:, :, sib], tbuf.at[c], at(core=sib))
    s_p = send(proj, pbuf.at[c], at(core=sib))
    s_g = send(gbuf.at[c], gbuf.at[c], at(core=sib))
    s_tp = send(table, tab.at[fs], at(dx=1))
    s_tm = send(table, tab.at[fs], at(dx=-1))
    s_ts = send(table, tab.at[fs], at(core=sib))

    l_t.wait()
    l_p.wait()

    def scaled(k, half):
        rows = tbuf[k, :, half].reshape(256, 256).astype(F32)
        return (rows * gbuf[k][0:1]).astype(BF)

    far, near = 1 - zh, zh
    for side, half in ((0, far), (1, near)):
        pacc[side] = dot(scaled(c, half), pbuf[c])
    s_t.wait_recv()
    s_p.wait_recv()
    s_g.wait_recv()

    def partial(side, half):
        total = pacc[side] + dot(scaled(sib, half), pbuf[sib])
        part[side] = total.astype(BF).reshape(4, 64, 1024)

    partial(0, far)
    s_f = []
    for k in range(2):
        rows = slice(32 * k, 32 * k + 32)
        s_f.append([
            send(part.at[0, x2, rows], fx.at[2, rows], at(dx=2)),
            send(part.at[0, x1, rows], fx.at[0, rows], at(dx=1)),
            send(part.at[0, x3, rows], fx.at[1, rows], at(dx=-1)),
        ])
    ones = jnp.ones((8, 256), BF)
    squares = jnp.zeros((8, 512), F32)
    for k in range(2):
        rows = tbuf[k].reshape(512, 256).astype(F32)
        sq = rows * rows
        hi = sq.astype(BF)
        lo = (sq - hi.astype(F32)).astype(BF)
        squares += lax.dot_general(ones, hi, NT, preferred_element_type=F32)
        squares += lax.dot_general(ones, lo, NT, preferred_element_type=F32)
    for k in range(4):
        ssp[k] = squares[:, 128 * k : 128 * (k + 1)]
    s_ss = [
        send(ssp.at[x1], ssr.at[0], at(dx=1)),
        send(ssp.at[x3], ssr.at[1], at(dx=-1)),
        send(ssp.at[x2], ssr.at[2], at(dx=2)),
    ]

    partial(1, near)

    def first_hop():
        return (
            send(part.at[1, x2, 0:32], rel.at[0], at(dx=1)),
            send(part.at[1, x2, 32:64], rel.at[1], at(dx=-1)),
            send(part.at[1, x1, 32:64], rx.at[0, 32:64], at(dx=1)),
            send(part.at[1, x3, 0:32], rx.at[1, 0:32], at(dx=-1)),
        )

    def second_hop():
        s_x[0].wait_recv()
        stg[0] = (part[1, x1, 0:32].astype(F32) + rel[0].astype(F32)).astype(BF)
        a = send(stg.at[0], rx.at[0, 0:32], at(dx=1))
        s_x[1].wait_recv()
        stg[1] = (part[1, x3, 32:64].astype(F32) + rel[1].astype(F32)).astype(BF)
        b = send(stg.at[1], rx.at[1, 32:64], at(dx=-1))
        return a, b

    def spread_near(place):
        up[place] = send_w(every, at_place(y, place), dy=1)
        down[place] = send_w(every, at_place(y, place), dy=-1)

    s_yn, s_sn = [], []

    def relay_near(place):
        up[place].wait_recv()
        s_yn.append(send_w(slice(0, 2), at_place(y3, place), dy=1))
        down[place].wait_recv()
        s_yn.append(send_w(slice(2, 4), at_place(y1, place), dy=-1))

    def share_near(yy):
        for first_place, count in ((0, 3), (6, 2)):
            rows = pl.ds(pl.multiple_of(yy * 256 + 32 * first_place, 32), 32 * count)
            s_sn.append(send_w(every, rows, core=sib))

    s_wy, s_ws = {}, {}

    def spread_far(r):
        s_wy[r] = [send_w(ring[r], far_rows(y), dy=1), send_w(ring[r], far_rows(y), dy=-1)]
        s_ws[r] = [send_w(ring[r], far_rows(y), core=sib)]

    def relay_far(r):
        s_wy[r][0].wait_recv()
        s_wy[r].append(send_w(ring[r], far_half(y3, 0), dy=1))
        s_ws[r].append(send_w(ring[r], far_rows(y3), core=sib))
        s_wy[r][1].wait_recv()
        s_wy[r].append(send_w(ring[r], far_half(y1, 1), dy=-1))
        s_ws[r].append(send_w(ring[r], far_rows(y1), core=sib))

    def finish_far(r):
        for copy in s_wy[r][2:]:
            copy.wait_recv()
        s_ws[r].append(send_w(ring[r], far_rows(y2), core=sib))

    def across(k):
        rows = slice(32 * k, 32 * k + 32)
        for copy in s_f[k]:
            copy.wait_recv()
        total = part[0, x, rows].astype(F32) + fx[0, rows].astype(F32)
        total = total + fx[1, rows].astype(F32) + fx[2, rows].astype(F32)
        zs[rows] = total.astype(BF)
        return send(zs.at[rows], zf.at[rows], at(dz=8))

    def pass_on(up_place, down_place):
        for k in range(2):
            for place, dz in ((up_place, 1), (down_place, -1)):
                from_z[place, k].wait_recv()
                if place not in (3, 5) or (place == 5) == (k == 0):
                    from_z[(place - dz) % 8, k] = along_z(place, dz, halves[k])

    pass_on(7, 1)
    spread_near(7)
    relay_near(0)
    fz = x * 4 + (1 - zh) * 2 + c
    s_tz.wait_recv()
    s_ty = [send(tab.at[fz, quarter], tab.at[fz, quarter], at(dy=k)) for k in (1, -1, 2)]
    spread_near(1)
    f3, f1 = x3 * 4 + zh * 2 + c, x1 * 4 + zh * 2 + c
    s_tp.wait_recv()
    s_tm.wait_recv()
    s_tx = [
        send(tab.at[f3, 0:32], tab.at[f3, 0:32], at(dx=1)),
        send(tab.at[f1, 32:64], tab.at[f1, 32:64], at(dx=-1)),
        send(tab.at[f3], tab.at[f3], at(core=sib)),
        send(tab.at[f1], tab.at[f1], at(core=sib)),
    ]
    pass_on(6, 2)
    spread_near(6)
    s_z = [across(0), across(1)]
    spread_near(2)
    s_x = first_hop()
    for copy in s_ty:
        copy.wait_recv()
    s_uz = [send(tab.at[fz], tab.at[fz], at(dx=k)) for k in (2, 1, -1)]
    s_us = [send(tab.at[fz], tab.at[fz], at(core=sib))]
    share_near(y)
    pass_on(5, 3)
    relay_near(7)
    relay_near(1)
    hops = second_hop()

    ids = codes[...]
    row = lax.broadcasted_iota(jnp.int32, (512, 64), 0)
    col = lax.broadcasted_iota(jnp.int32, (512, 64), 1)
    spread = (row // 8 == col).astype(BF)
    high = (ids // 32).astype(F32).astype(BF)
    low = lax.rem(ids, 32).astype(F32).astype(BF)
    high = lax.dot_general(spread, high, NT, preferred_element_type=F32)
    low = lax.dot_general(spread, low, NT, preferred_element_type=F32)
    row8 = lax.broadcasted_iota(jnp.int32, (512, 8), 0)
    col8 = lax.broadcasted_iota(jnp.int32, (512, 8), 1)
    picked = jnp.where(lax.rem(row8, 8) == col8, high * 32.0 + low, 0.0)
    id_col = jnp.sum(picked, axis=1, keepdims=True).astype(jnp.int32)

    for copy in s_ss:
        copy.wait_recv()
    ssx[...] = ssp[x] + ssr[0] + ssr[1] + ssr[2]
    s_ssz = send(ssx, ssz, at(dz=8))
    f2 = x2 * 4 + zh * 2 + c
    s_tx[0].wait_recv()
    s_tx[1].wait_recv()
    s_tx.append(send(tab.at[f2], tab.at[f2], at(core=sib)))
    relay_near(6)
    relay_near(2)
    for copy, xx in zip(s_uz, (x2, x3, x1)):
        copy.wait_recv()
        ref = tab.at[xx * 4 + (1 - zh) * 2 + c]
        s_us.append(send(ref, ref, at(core=sib)))
    from_z[4, 0].wait_recv()
    from_z[4, 1].wait_recv()
    spread_far(0)
    spread_far(1)
    l_tab.wait()
    for copy in [s_ts] + s_tx[2:] + s_us:
        copy.wait_recv()

    lanes = lax.broadcasted_iota(jnp.int32, (128, 1024), 1)
    whole_table = tab[...].reshape(1024, 1024)
    for t in range(4):
        onehot = (lanes == id_col[128 * t : 128 * (t + 1)]).astype(F32).astype(BF)
        emb[128 * t : 128 * (t + 1)] = dot(onehot, whole_table).astype(BF)

    relay_far(0)
    spread_far(2)

    for copy in s_x[2:] + hops:
        copy.wait_recv()
    total = part[1, x].astype(F32) + rx[0].astype(F32) + rx[1].astype(F32)
    s_ssz.wait_recv()
    sums = ssx[...] + ssz[...]
    lane = lax.broadcasted_iota(jnp.int32, (64, 128), 1)
    sub = lax.broadcasted_iota(jnp.int32, (64, 128), 0)
    sum_col = jnp.sum(
        jnp.where(lane == sub + 64 * zh, sums[0:1], 0.0), axis=1, keepdims=True
    )
    inv_rms = lax.rsqrt(sum_col * (1.0 / 4096.0) + 1e-05)
    for copy in s_z:
        copy.wait_recv()
    context = ((total + zf[...].astype(F32)) * inv_rms).astype(BF).astype(F32)
    depth_gain = dgain[...].astype(F32).reshape(1, 1024)
    turn = lax.rem(256 - 32 * zl, 256)
    for t in range(4):
        rows = slice(128 * t, 128 * (t + 1))
        wide = jnp.broadcast_to(context[16 * t : 16 * (t + 1)][:, None, :], (16, 8, 1024))
        value = wide.reshape(128, 1024) + emb[rows].astype(F32)
        inv = lax.rsqrt(jnp.mean(value * value, axis=-1, keepdims=True) + 1e-05)
        stream[rows] = value
        value = value * inv * depth_gain
        for k in range(4):
            part_k = pltpu.roll(value[:, 256 * k : 256 * (k + 1)], turn, 1)
            normed[rows, 256 * k : 256 * (k + 1)] = part_k.astype(BF)
    relay_far(1)
    spread_far(3)
    for copy in s_yn:
        copy.wait_recv()
    for yy in (y1, y2, y3):
        share_near(yy)
    finish_far(0)
    relay_far(2)
    finish_far(1)

    first = lax.broadcasted_iota(jnp.int32, (128, 128), 1) < 64
    frame_of_lane = lax.broadcasted_iota(jnp.int32, (8, 128), 1) // 8
    position = lax.broadcasted_iota(jnp.int32, (128, 128), 0)
    query = lax.broadcasted_iota(jnp.int32, (128, 128), 1)
    allowed = lax.rem(position, 8) <= lax.rem(query, 8)
    def by_head(a):
        a = a.astype(F32)
        return jnp.concatenate(
            [jnp.where(first, a, 0.0).astype(BF), jnp.where(first, 0.0, a).astype(BF)], axis=0
        )

    def attend(r):
        for t in range(2):
            rows = slice(256 * t, 256 * (t + 1))
            qkv[rows] = dot(normed[rows], wb[ring[r]]).astype(BF)
        for t in range(4):
            rows = slice(128 * t, 128 * (t + 1))
            for b in range(2):
                q = qkv[rows, 384 * b : 384 * b + 128]
                k = by_head(qkv[rows, 384 * b + 128 : 384 * b + 256])
                scores = lax.dot_general(k, q, NT, preferred_element_type=F32)
                for h in range(2):
                    own = scores[128 * h : 128 * h + 8]
                    for f in range(1, 16):
                        own = jnp.where(
                            frame_of_lane == f, scores[128 * h + 8 * f : 128 * h + 8 * f + 8], own
                        )
                    unit = t * 4 + b * 2 + h
                    comp[8 * unit : 8 * unit + 8] = own
        scores = jnp.where(allowed, comp[...] * 0.125, -1e30).reshape(16, 8, 128)
        e = jnp.exp(scores - jnp.max(scores, axis=1, keepdims=True))
        weights = (e / jnp.sum(e, axis=1, keepdims=True)).reshape(128, 128)
        for t in range(4):
            rows = slice(128 * t, 128 * (t + 1))
            for b in range(2):
                wide = []
                for unit in (t * 4 + b * 2, t * 4 + b * 2 + 1):
                    own = weights[8 * unit : 8 * unit + 8]
                    wide += [jnp.where(frame_of_lane == f, own, 0.0) for f in range(16)]
                wide = jnp.concatenate(wide, axis=0).astype(BF)
                v = by_head(qkv[rows, 384 * b + 256 : 384 * b + 384])
                mixed[rows, 256 * r + 128 * b : 256 * r + 128 * b + 128] = lax.dot_general(
                    wide, v, TN, preferred_element_type=F32
                ).astype(BF)

    for copy in l_out:
        copy.wait()
    for copy in s_sn:
        copy.wait_recv()
    for r in range(4):
        if r == 1:
            finish_far(2)
            relay_far(3)
        if r == 2:
            finish_far(3)
        for copy in s_ws[r]:
            copy.wait_recv()
        attend(r)
    stores = []
    for t in range(4):
        rows = slice(128 * t, 128 * (t + 1))
        outb[rows] = (stream[rows] + dot(mixed[rows], doutb[...])).astype(BF)
        stores.append(load(outb.at[rows], out.at[rows]))
    for copy in stores:
        copy.wait()

    for copy in started:
        copy.wait_send()


def per_device(
    temporal_out, norm_gain, input_proj, code_table, depth_gain, depth_proj, depth_out, code_ids
):
    vmem = pl.BlockSpec(memory_space=pltpu.VMEM)
    hbm = pl.BlockSpec(memory_space=pl.ANY)
    scratch = [
        ((2, 4, 2, 64, 256), BF),
        ((2, 256, 1024), BF),
        ((2, 8, 256), F32),
        ((2, 256, 1024), F32),
        ((2, 4, 64, 1024), BF),
        ((2, 32, 1024), BF),
        ((2, 64, 1024), BF),
        ((2, 32, 1024), BF),
        ((3, 64, 1024), BF),
        ((64, 1024), BF),
        ((64, 1024), BF),
        ((4, 8, 128), F32),
        ((3, 8, 128), F32),
        ((8, 128), F32),
        ((8, 128), F32),
        ((16, 64, 1024), BF),
        ((512, 1024), BF),
        ((512, 1024), BF),
        ((512, 1024), F32),
        ((4, 1024, 768), BF),
        ((512, 768), BF),
        ((128, 128), F32),
        ((512, 1024), BF),
        ((1024, 1024), BF),
        ((512, 1024), BF),
    ]
    operands = (
        temporal_out.reshape(4, 2, 2, 64, 256),
        norm_gain,
        input_proj,
        code_table,
        depth_gain,
        depth_proj,
        depth_out,
        code_ids.reshape(64, 8).T,
    )
    result = pl.pallas_call(
        kernel,
        out_shape=jax.ShapeDtypeStruct((512, 1024), BF),
        in_specs=[hbm, vmem, hbm, hbm, vmem, hbm, hbm, vmem],
        out_specs=hbm,
        scratch_shapes=[pltpu.VMEM(shape, dtype) for shape, dtype in scratch]
        + [
            pltpu.SemaphoreType.DMA((N_REMOTE,)),
            pltpu.SemaphoreType.DMA((N_REMOTE,)),
            pltpu.SemaphoreType.DMA((32,)),
        ],
        compiler_params=pltpu.CompilerParams(
            collective_id=0, has_side_effects=True, vmem_limit_bytes=40 * 1024 * 1024
        ),
        cost_estimate=pl.CostEstimate(
            flops=6_500_000_000, bytes_accessed=6_000_000, transcendentals=2_000_000
        ),
    )(*(pltpu.with_memory_space_constraint(a, pltpu.HBM) for a in operands))
    return result.reshape(1, 1, 64, 8, 1024)


def solution(mesh):
    placed = (
        P("frame", "fsdp"),
        P("fsdp"),
        P("fsdp", None),
        P("fsdp", None),
        P(),
        P("frame", None),
        P(),
        P("frame", "fsdp", None, None),
    )
    return jax.shard_map(
        per_device,
        mesh=mesh,
        in_specs=placed,
        out_specs=P("frame", "fsdp", None, None, None),
        check_vma=False,
    )
```

```python
import functools

import jax
import jax.numpy as jnp
from jax import lax
from jax.experimental import pallas as pl
from jax.experimental.pallas import tpu as pltpu
from jax.sharding import PartitionSpec as P

BF = jnp.bfloat16
F32 = jnp.float32
MESH = pl.DeviceIdType.MESH
NT = (((1,), (1,)), ((), ()))
TN = (((0,), (0,)), ((), ()))
N_REMOTE = 128


def dot(a, b):
    return jnp.dot(a, b, preferred_element_type=F32)


def kernel(
    temporal, gain, proj, table, dgain, dproj, dout, codes,
    out,
    tbuf, pbuf, gbuf, pacc, part, rel, rx, stg, fx, zs, zf,
    ssp, ssr, ssx, ssz,
    tab, emb, normed, stream,
    wb, qkv, comp, mixed, doutb, outb,
    ssem, rsem, lsem,
):
    fs = lax.axis_index("fsdp")
    fr = lax.axis_index("frame")
    x, zh, c = fs // 4, lax.rem(fs // 2, 2), lax.rem(fs, 2)
    y, zl = fr // 8, lax.rem(fr, 8)
    z = zh * 8 + zl
    sib = 1 - c

    def at(dx=0, dy=0, dz=0, core=None):
        tx, ty, tz = lax.rem(x + dx + 4, 4), lax.rem(y + dy + 4, 4), lax.rem(z + dz + 16, 16)
        tc = c if core is None else core
        return (tx * 4 + (tz // 8) * 2 + tc, ty * 8 + lax.rem(tz, 8))

    x1, x2, x3 = lax.rem(x + 1, 4), lax.rem(x + 2, 4), lax.rem(x + 3, 4)
    y1, y2, y3 = lax.rem(y + 1, 4), lax.rem(y + 2, 4), lax.rem(y + 3, 4)

    started = []

    def send(src, dst, dev):
        index = len(started)
        copy = pltpu.make_async_remote_copy(
            src_ref=src, dst_ref=dst, send_sem=ssem.at[index], recv_sem=rsem.at[index],
            device_id=dev, device_id_type=MESH,
        )
        copy.start()
        started.append(copy)
        return copy

    locals_ = []

    def load(src, dst):
        copy = pltpu.make_async_copy(src, dst, lsem.at[len(locals_)])
        copy.start()
        locals_.append(copy)
        return copy

    mine = pl.ds(pl.multiple_of(c * 384, 128), 384)
    ring = [lax.rem(x + k, 4) for k in (0, 3, 1, 2)]

    def at_place(yy, place):
        return pl.ds(pl.multiple_of(yy * 256 + 32 * place, 32), 32)

    def far_rows(yy):
        return at_place(yy, 4)

    def far_half(yy, k):
        return pl.ds(pl.multiple_of(yy * 256 + 128 + 16 * k, 16), 16)

    l_w = [
        load(
            dproj.at[:, pl.ds(pl.multiple_of(k * 1024 + (2 * xx + c) * 128, 128), 128)],
            wb.at[xx, at_place(y, 0), pl.ds(pl.multiple_of(c * 384 + k * 128, 128), 128)],
        )
        for xx in range(4)
        for k in range(3)
    ]
    l_t = load(temporal.at[:, :, c], tbuf.at[c])
    l_p = load(proj, pbuf.at[c])
    l_tab = load(table, tab.at[fs])
    l_out = [
        load(dout.at[pl.ds(pl.multiple_of(ring[r] * 256, 256), 256)], doutb.at[256 * r : 256 * r + 256])
        for r in range(4)
    ]
    gbuf[c] = jnp.broadcast_to(gain[...].astype(F32).reshape(1, 256), (8, 256))

    partners = [at(core=sib)]
    partners += [at(dx=k) for k in (1, -1, 2)] + [at(dy=k) for k in (1, -1, 2)]
    partners += [at(dz=k) for k in (1, -1, 4, -4, 8)]
    barrier = pltpu.get_barrier_semaphore()
    partners.append((x * 4 + (1 - zh) * 2 + c, y * 8 + 7 - zl))
    for partner in partners:
        pl.semaphore_signal(barrier, inc=1, device_id=partner, device_id_type=MESH)
    pl.semaphore_wait(barrier, len(partners))

    quarter = pl.ds(pl.multiple_of(y * 16, 16), 16)
    mirror = (x * 4 + (1 - zh) * 2 + c, y * 8 + 7 - zl)
    s_tz = send(table.at[quarter], tab.at[fs, quarter], mirror)
    for copy in l_w:
        copy.wait()

    def send_w(xx, rows, **to):
        ref = wb.at[xx, rows, mine]
        return send(ref, ref, at(**to))

    every = slice(0, 4)

    def along_z(place, dz, pieces=slice(0, 4)):
        return send(
            wb.at[pieces, at_place(y, place), mine],
            wb.at[pieces, at_place(y, (place - dz) % 8), mine],
            at(dz=dz),
        )

    halves = (slice(0, 2), slice(2, 4))
    from_z = {}
    for k in range(2):
        for place, dz in ((7, 1), (1, -1)):
            from_z[place, k] = along_z(0, dz, halves[k])
    up = {0: send_w(every, at_place(y, 0), dy=1)}
    down = {0: send_w(every, at_place(y, 0), dy=-1)}
    far_z = [
        send(wb.at[x, at_place(y, 0), mine], wb.at[x, at_place(y, -k % 8), mine], at(dz=k))
        for k in (4,)
    ]
    s_t = send(temporal.at[:, :, sib], tbuf.at[c], at(core=sib))
    s_p = send(proj, pbuf.at[c], at(core=sib))
    s_g = send(gbuf.at[c], gbuf.at[c], at(core=sib))
    s_tp = send(table, tab.at[fs], at(dx=1))
    s_tm = send(table, tab.at[fs], at(dx=-1))
    s_ts = send(table, tab.at[fs], at(core=sib))

    l_t.wait()
    l_p.wait()

    def scaled(k, half):
        rows = tbuf[k, :, half].reshape(256, 256).astype(F32)
        return (rows * gbuf[k][0:1]).astype(BF)

    far, near = 1 - zh, zh
    for side, half in ((0, far), (1, near)):
        pacc[side] = dot(scaled(c, half), pbuf[c])
    s_t.wait_recv()
    s_p.wait_recv()
    s_g.wait_recv()

    def partial(side, half):
        total = pacc[side] + dot(scaled(sib, half), pbuf[sib])
        part[side] = total.astype(BF).reshape(4, 64, 1024)

    partial(0, far)
    s_f = []
    for k in range(2):
        rows = slice(32 * k, 32 * k + 32)
        s_f.append([
            send(part.at[0, x2, rows], fx.at[2, rows], at(dx=2)),
            send(part.at[0, x1, rows], fx.at[0, rows], at(dx=1)),
            send(part.at[0, x3, rows], fx.at[1, rows], at(dx=-1)),
        ])
    ones = jnp.ones((8, 256), BF)
    squares = jnp.zeros((8, 512), F32)
    for k in range(2):
        rows = tbuf[k].reshape(512, 256).astype(F32)
        sq = rows * rows
        hi = sq.astype(BF)
        lo = (sq - hi.astype(F32)).astype(BF)
        squares += lax.dot_general(ones, hi, NT, preferred_element_type=F32)
        squares += lax.dot_general(ones, lo, NT, preferred_element_type=F32)
    for k in range(4):
        ssp[k] = squares[:, 128 * k : 128 * (k + 1)]
    s_ss = [
        send(ssp.at[x1], ssr.at[0], at(dx=1)),
        send(ssp.at[x3], ssr.at[1], at(dx=-1)),
        send(ssp.at[x2], ssr.at[2], at(dx=2)),
    ]

    partial(1, near)

    def first_hop():
        return (
            send(part.at[1, x2, 0:32], rel.at[0], at(dx=1)),
            send(part.at[1, x2, 32:64], rel.at[1], at(dx=-1)),
            send(part.at[1, x1, 32:64], rx.at[0, 32:64], at(dx=1)),
            send(part.at[1, x3, 0:32], rx.at[1, 0:32], at(dx=-1)),
        )

    def second_hop():
        s_x[0].wait_recv()
        stg[0] = (part[1, x1, 0:32].astype(F32) + rel[0].astype(F32)).astype(BF)
        a = send(stg.at[0], rx.at[0, 0:32], at(dx=1))
        s_x[1].wait_recv()
        stg[1] = (part[1, x3, 32:64].astype(F32) + rel[1].astype(F32)).astype(BF)
        b = send(stg.at[1], rx.at[1, 32:64], at(dx=-1))
        return a, b

    def spread_near(place):
        up[place] = send_w(every, at_place(y, place), dy=1)
        down[place] = send_w(every, at_place(y, place), dy=-1)

    s_yn, s_sn = [], []

    def relay_near(place):
        up[place].wait_recv()
        s_yn.append(send_w(slice(0, 2), at_place(y3, place), dy=1))
        down[place].wait_recv()
        s_yn.append(send_w(slice(2, 4), at_place(y1, place), dy=-1))

    def share_near(yy):
        for first_place, count in ((0, 4), (5, 3)):
            rows = pl.ds(pl.multiple_of(yy * 256 + 32 * first_place, 32), 32 * count)
            s_sn.append(send_w(every, rows, core=sib))

    s_wy, s_ws = {}, {}

    def spread_far(r):
        s_wy[r] = [send_w(ring[r], far_rows(y), dy=1), send_w(ring[r], far_rows(y), dy=-1)]
        s_ws[r] = [send_w(ring[r], far_rows(y), core=sib)]

    def relay_far(r):
        s_wy[r][0].wait_recv()
        s_wy[r].append(send_w(ring[r], far_half(y3, 0), dy=1))
        s_ws[r].append(send_w(ring[r], far_rows(y3), core=sib))
        s_wy[r][1].wait_recv()
        s_wy[r].append(send_w(ring[r], far_half(y1, 1), dy=-1))
        s_ws[r].append(send_w(ring[r], far_rows(y1), core=sib))

    def finish_far(r):
        for copy in s_wy[r][2:]:
            copy.wait_recv()
        s_ws[r].append(send_w(ring[r], far_rows(y2), core=sib))

    def across(k):
        rows = slice(32 * k, 32 * k + 32)
        for copy in s_f[k]:
            copy.wait_recv()
        total = part[0, x, rows].astype(F32) + fx[0, rows].astype(F32)
        total = total + fx[1, rows].astype(F32) + fx[2, rows].astype(F32)
        zs[rows] = total.astype(BF)
        return send(zs.at[rows], zf.at[rows], at(dz=8))

    def pass_on(up_place, down_place):
        for k in range(2):
            for place, dz in ((up_place, 1), (down_place, -1)):
                from_z[place, k].wait_recv()
                from_z[(place - dz) % 8, k] = along_z(place, dz, halves[k])

    pass_on(7, 1)
    spread_near(7)
    spread_near(1)
    relay_near(0)
    f3, f1 = x3 * 4 + zh * 2 + c, x1 * 4 + zh * 2 + c
    s_tp.wait_recv()
    s_tm.wait_recv()
    s_tx = [
        send(tab.at[f3, 0:32], tab.at[f3, 0:32], at(dx=1)),
        send(tab.at[f1, 32:64], tab.at[f1, 32:64], at(dx=-1)),
        send(tab.at[f3], tab.at[f3], at(core=sib)),
        send(tab.at[f1], tab.at[f1], at(core=sib)),
    ]
    fz = x * 4 + (1 - zh) * 2 + c
    s_tz.wait_recv()
    s_ty = [send(tab.at[fz, quarter], tab.at[fz, quarter], at(dy=k)) for k in (1, -1, 2)]
    pass_on(6, 2)
    spread_near(6)
    s_z = [across(0)]
    for copy in s_ss:
        copy.wait_recv()
    ssx[...] = ssp[x] + ssr[0] + ssr[1] + ssr[2]
    s_ssz = send(ssx, ssz, at(dz=8))
    s_z.append(across(1))
    far_z[0].wait_recv()
    s_wx = [send_w(x, far_rows(y), dx=k) for k in (1, -1, 2)]
    s_x = first_hop()
    for copy in s_ty:
        copy.wait_recv()
    s_uz = [send(tab.at[fz], tab.at[fz], at(dx=k)) for k in (2, 1, -1)]
    s_us = [send(tab.at[fz], tab.at[fz], at(core=sib))]
    relay_near(7)
    spread_near(2)
    relay_near(1)

    ids = codes[...]
    row = lax.broadcasted_iota(jnp.int32, (512, 64), 0)
    col = lax.broadcasted_iota(jnp.int32, (512, 64), 1)
    spread = (row // 8 == col).astype(BF)
    high = (ids // 32).astype(F32).astype(BF)
    low = lax.rem(ids, 32).astype(F32).astype(BF)
    high = lax.dot_general(spread, high, NT, preferred_element_type=F32)
    low = lax.dot_general(spread, low, NT, preferred_element_type=F32)
    row8 = lax.broadcasted_iota(jnp.int32, (512, 8), 0)
    col8 = lax.broadcasted_iota(jnp.int32, (512, 8), 1)
    picked = jnp.where(lax.rem(row8, 8) == col8, high * 32.0 + low, 0.0)
    id_col = jnp.sum(picked, axis=1, keepdims=True).astype(jnp.int32)

    hops = second_hop()
    f2 = x2 * 4 + zh * 2 + c
    s_tx[0].wait_recv()
    s_tx[1].wait_recv()
    s_tx.append(send(tab.at[f2], tab.at[f2], at(core=sib)))
    for place in (5, 3):
        for k in range(2):
            from_z[place, k].wait_recv()
        spread_near(place)
    relay_near(6)
    share_near(y)
    spread_far(0)
    for r in (1, 2, 3):
        s_wx[r - 1].wait_recv()
        spread_far(r)
    for copy, xx in zip(s_uz, (x2, x3, x1)):
        copy.wait_recv()
        ref = tab.at[xx * 4 + (1 - zh) * 2 + c]
        s_us.append(send(ref, ref, at(core=sib)))
    relay_near(2)
    l_tab.wait()
    for copy in [s_ts] + s_tx[2:] + s_us:
        copy.wait_recv()

    lanes = lax.broadcasted_iota(jnp.int32, (128, 1024), 1)
    whole_table = tab[...].reshape(1024, 1024)
    for t in range(4):
        onehot = (lanes == id_col[128 * t : 128 * (t + 1)]).astype(F32).astype(BF)
        emb[128 * t : 128 * (t + 1)] = dot(onehot, whole_table).astype(BF)

    relay_near(5)
    relay_near(3)
    share_near(y1)
    share_near(y3)

    for copy in s_x[2:] + hops:
        copy.wait_recv()
    total = part[1, x].astype(F32) + rx[0].astype(F32) + rx[1].astype(F32)
    s_ssz.wait_recv()
    sums = ssx[...] + ssz[...]
    lane = lax.broadcasted_iota(jnp.int32, (64, 128), 1)
    sub = lax.broadcasted_iota(jnp.int32, (64, 128), 0)
    sum_col = jnp.sum(
        jnp.where(lane == sub + 64 * zh, sums[0:1], 0.0), axis=1, keepdims=True
    )
    inv_rms = lax.rsqrt(sum_col * (1.0 / 4096.0) + 1e-05)
    for copy in s_z:
        copy.wait_recv()
    context = ((total + zf[...].astype(F32)) * inv_rms).astype(BF).astype(F32)
    depth_gain = dgain[...].astype(F32).reshape(1, 1024)
    turn = lax.rem(256 - 32 * zl, 256)
    for t in range(4):
        rows = slice(128 * t, 128 * (t + 1))
        wide = jnp.broadcast_to(context[16 * t : 16 * (t + 1)][:, None, :], (16, 8, 1024))
        value = wide.reshape(128, 1024) + emb[rows].astype(F32)
        inv = lax.rsqrt(jnp.mean(value * value, axis=-1, keepdims=True) + 1e-05)
        stream[rows] = value
        value = value * inv * depth_gain
        for k in range(4):
            part_k = pltpu.roll(value[:, 256 * k : 256 * (k + 1)], turn, 1)
            normed[rows, 256 * k : 256 * (k + 1)] = part_k.astype(BF)
    relay_far(0)
    relay_far(1)
    for copy in s_yn:
        copy.wait_recv()
    share_near(y2)
    relay_far(2)
    relay_far(3)
    finish_far(0)
    finish_far(1)

    first = lax.broadcasted_iota(jnp.int32, (128, 128), 1) < 64
    frame_of_lane = lax.broadcasted_iota(jnp.int32, (8, 128), 1) // 8
    position = lax.broadcasted_iota(jnp.int32, (128, 128), 0)
    query = lax.broadcasted_iota(jnp.int32, (128, 128), 1)
    allowed = lax.rem(position, 8) <= lax.rem(query, 8)
    def by_head(a):
        a = a.astype(F32)
        return jnp.concatenate(
            [jnp.where(first, a, 0.0).astype(BF), jnp.where(first, 0.0, a).astype(BF)], axis=0
        )

    def attend(r):
        for t in range(2):
            rows = slice(256 * t, 256 * (t + 1))
            qkv[rows] = dot(normed[rows], wb[ring[r]]).astype(BF)
        for t in range(4):
            rows = slice(128 * t, 128 * (t + 1))
            for b in range(2):
                q = qkv[rows, 384 * b : 384 * b + 128]
                k = by_head(qkv[rows, 384 * b + 128 : 384 * b + 256])
                scores = lax.dot_general(k, q, NT, preferred_element_type=F32)
                for h in range(2):
                    own = scores[128 * h : 128 * h + 8]
                    for f in range(1, 16):
                        own = jnp.where(
                            frame_of_lane == f, scores[128 * h + 8 * f : 128 * h + 8 * f + 8], own
                        )
                    unit = t * 4 + b * 2 + h
                    comp[8 * unit : 8 * unit + 8] = own
        scores = jnp.where(allowed, comp[...] * 0.125, -1e30).reshape(16, 8, 128)
        e = jnp.exp(scores - jnp.max(scores, axis=1, keepdims=True))
        weights = (e / jnp.sum(e, axis=1, keepdims=True)).reshape(128, 128)
        for t in range(4):
            rows = slice(128 * t, 128 * (t + 1))
            for b in range(2):
                wide = []
                for unit in (t * 4 + b * 2, t * 4 + b * 2 + 1):
                    own = weights[8 * unit : 8 * unit + 8]
                    wide += [jnp.where(frame_of_lane == f, own, 0.0) for f in range(16)]
                wide = jnp.concatenate(wide, axis=0).astype(BF)
                v = by_head(qkv[rows, 384 * b + 256 : 384 * b + 384])
                mixed[rows, 256 * r + 128 * b : 256 * r + 128 * b + 128] = lax.dot_general(
                    wide, v, TN, preferred_element_type=F32
                ).astype(BF)

    for copy in l_out:
        copy.wait()
    for copy in s_sn:
        copy.wait_recv()
    for r in range(4):
        if 0 < r < 3:
            finish_far(r + 1)
        if r == 3:
            for t in range(4):
                rows = slice(128 * t, 128 * (t + 1))
                stream[rows] = stream[rows] + dot(mixed[rows, :768], doutb[:768])
        for copy in s_ws[r]:
            copy.wait_recv()
        attend(r)
    stores = []
    for t in range(4):
        rows = slice(128 * t, 128 * (t + 1))
        outb[rows] = (stream[rows] + dot(mixed[rows, 768:], doutb[768:])).astype(BF)
        stores.append(load(outb.at[rows], out.at[rows]))
    for copy in stores:
        copy.wait()

    for copy in started:
        copy.wait_send()


def per_device(
    temporal_out, norm_gain, input_proj, code_table, depth_gain, depth_proj, depth_out, code_ids
):
    vmem = pl.BlockSpec(memory_space=pltpu.VMEM)
    hbm = pl.BlockSpec(memory_space=pl.ANY)
    scratch = [
        ((2, 4, 2, 64, 256), BF),
        ((2, 256, 1024), BF),
        ((2, 8, 256), F32),
        ((2, 256, 1024), F32),
        ((2, 4, 64, 1024), BF),
        ((2, 32, 1024), BF),
        ((2, 64, 1024), BF),
        ((2, 32, 1024), BF),
        ((3, 64, 1024), BF),
        ((64, 1024), BF),
        ((64, 1024), BF),
        ((4, 8, 128), F32),
        ((3, 8, 128), F32),
        ((8, 128), F32),
        ((8, 128), F32),
        ((16, 64, 1024), BF),
        ((512, 1024), BF),
        ((512, 1024), BF),
        ((512, 1024), F32),
        ((4, 1024, 768), BF),
        ((512, 768), BF),
        ((128, 128), F32),
        ((512, 1024), BF),
        ((1024, 1024), BF),
        ((512, 1024), BF),
    ]
    operands = (
        temporal_out.reshape(4, 2, 2, 64, 256),
        norm_gain,
        input_proj,
        code_table,
        depth_gain,
        depth_proj,
        depth_out,
        code_ids.reshape(64, 8).T,
    )
    result = pl.pallas_call(
        kernel,
        out_shape=jax.ShapeDtypeStruct((512, 1024), BF),
        in_specs=[hbm, vmem, hbm, hbm, vmem, hbm, hbm, vmem],
        out_specs=hbm,
        scratch_shapes=[pltpu.VMEM(shape, dtype) for shape, dtype in scratch]
        + [
            pltpu.SemaphoreType.DMA((N_REMOTE,)),
            pltpu.SemaphoreType.DMA((N_REMOTE,)),
            pltpu.SemaphoreType.DMA((32,)),
        ],
        compiler_params=pltpu.CompilerParams(
            collective_id=0, has_side_effects=True, vmem_limit_bytes=40 * 1024 * 1024
        ),
        cost_estimate=pl.CostEstimate(
            flops=6_500_000_000, bytes_accessed=6_000_000, transcendentals=2_000_000
        ),
    )(*(pltpu.with_memory_space_constraint(a, pltpu.HBM) for a in operands))
    return result.reshape(1, 1, 64, 8, 1024)


def solution(mesh):
    placed = (
        P("frame", "fsdp"),
        P("fsdp"),
        P("fsdp", None),
        P("fsdp", None),
        P(),
        P("frame", None),
        P(),
        P("frame", "fsdp", None, None),
    )
    return jax.shard_map(
        per_device,
        mesh=mesh,
        in_specs=placed,
        out_specs=P("frame", "fsdp", None, None, None),
        check_vma=False,
    )
```

```python
import functools

import jax
import jax.numpy as jnp
from jax import lax
from jax.experimental import pallas as pl
from jax.experimental.pallas import tpu as pltpu
from jax.sharding import PartitionSpec as P

BF = jnp.bfloat16
F32 = jnp.float32
MESH = pl.DeviceIdType.MESH
NT = (((1,), (1,)), ((), ()))
TN = (((0,), (0,)), ((), ()))
N_REMOTE = 128


def dot(a, b):
    return jnp.dot(a, b, preferred_element_type=F32)


def kernel(
    temporal, gain, proj, table, dgain, dproj, dout, codes,
    out,
    tbuf, pbuf, gbuf, pacc, part, rel, rx, stg, fx, zs, zf,
    ssp, ssr, ssx, ssz,
    tab, emb, normed, stream,
    wb, early, qkv, comp, mixed, doutb, outb,
    ssem, rsem, lsem,
):
    fs = lax.axis_index("fsdp")
    fr = lax.axis_index("frame")
    x, zh, c = fs // 4, lax.rem(fs // 2, 2), lax.rem(fs, 2)
    y, zl = fr // 8, lax.rem(fr, 8)
    z = zh * 8 + zl
    sib = 1 - c

    def at(dx=0, dy=0, dz=0, core=None):
        tx, ty, tz = lax.rem(x + dx + 4, 4), lax.rem(y + dy + 4, 4), lax.rem(z + dz + 16, 16)
        tc = c if core is None else core
        return (tx * 4 + (tz // 8) * 2 + tc, ty * 8 + lax.rem(tz, 8))

    x1, x2, x3 = lax.rem(x + 1, 4), lax.rem(x + 2, 4), lax.rem(x + 3, 4)
    y1, y2, y3 = lax.rem(y + 1, 4), lax.rem(y + 2, 4), lax.rem(y + 3, 4)

    started = []

    def send(src, dst, dev):
        index = len(started)
        copy = pltpu.make_async_remote_copy(
            src_ref=src, dst_ref=dst, send_sem=ssem.at[index], recv_sem=rsem.at[index],
            device_id=dev, device_id_type=MESH,
        )
        copy.start()
        started.append(copy)
        return copy

    locals_ = []

    def load(src, dst):
        copy = pltpu.make_async_copy(src, dst, lsem.at[len(locals_)])
        copy.start()
        locals_.append(copy)
        return copy

    mine = pl.ds(pl.multiple_of(c * 384, 128), 384)
    ring = [lax.rem(x + k, 4) for k in (0, 3, 1, 2)]

    def at_place(yy, place):
        return pl.ds(pl.multiple_of(yy * 256 + 32 * place, 32), 32)

    def far_rows(yy):
        return at_place(yy, 4)

    def far_half(yy, k):
        return pl.ds(pl.multiple_of(yy * 256 + 128 + 16 * k, 16), 16)

    l_w = [
        load(
            dproj.at[:, pl.ds(pl.multiple_of(k * 1024 + (2 * xx + c) * 128, 128), 128)],
            wb.at[xx, at_place(y, 0), pl.ds(pl.multiple_of(c * 384 + k * 128, 128), 128)],
        )
        for xx in range(4)
        for k in range(3)
    ]
    l_t = load(temporal.at[:, :, c], tbuf.at[c])
    l_p = load(proj, pbuf.at[c])
    l_tab = load(table, tab.at[fs])
    l_out = [
        load(dout.at[pl.ds(pl.multiple_of(ring[r] * 256, 256), 256)], doutb.at[256 * r : 256 * r + 256])
        for r in range(4)
    ]
    gbuf[c] = jnp.broadcast_to(gain[...].astype(F32).reshape(1, 256), (8, 256))

    partners = [at(core=sib)]
    partners += [at(dx=k) for k in (1, -1, 2)] + [at(dy=k) for k in (1, -1, 2)]
    partners += [at(dz=k) for k in (1, -1, 4, -4, 8)]
    barrier = pltpu.get_barrier_semaphore()
    partners.append((x * 4 + (1 - zh) * 2 + c, y * 8 + 7 - zl))
    for partner in partners:
        pl.semaphore_signal(barrier, inc=1, device_id=partner, device_id_type=MESH)
    pl.semaphore_wait(barrier, len(partners))

    quarter = pl.ds(pl.multiple_of(y * 16, 16), 16)
    mirror = (x * 4 + (1 - zh) * 2 + c, y * 8 + 7 - zl)
    s_tz = send(table.at[quarter], tab.at[fs, quarter], mirror)
    for copy in l_w:
        copy.wait()

    def send_w(xx, rows, **to):
        ref = wb.at[xx, rows, mine]
        return send(ref, ref, at(**to))

    every = slice(0, 4)

    def along_z(place, dz, pieces=slice(0, 4)):
        return send(
            wb.at[pieces, at_place(y, place), mine],
            wb.at[pieces, at_place(y, (place - dz) % 8), mine],
            at(dz=dz),
        )

    halves = (slice(0, 2), slice(2, 4))
    from_z = {}
    for k in range(2):
        for place, dz in ((7, 1), (1, -1)):
            from_z[place, k] = along_z(0, dz, halves[k])
    up = {0: send_w(every, at_place(y, 0), dy=1)}
    down = {0: send_w(every, at_place(y, 0), dy=-1)}
    far_z = [
        send(wb.at[x, at_place(y, 0), mine], wb.at[x, at_place(y, -k % 8), mine], at(dz=k))
        for k in (4,)
    ]
    s_t = send(temporal.at[:, :, sib], tbuf.at[c], at(core=sib))
    s_p = send(proj, pbuf.at[c], at(core=sib))
    s_g = send(gbuf.at[c], gbuf.at[c], at(core=sib))
    s_tp = send(table, tab.at[fs], at(dx=1))
    s_tm = send(table, tab.at[fs], at(dx=-1))
    s_ts = send(table, tab.at[fs], at(core=sib))

    l_t.wait()
    l_p.wait()

    def scaled(k, half):
        rows = tbuf[k, :, half].reshape(256, 256).astype(F32)
        return (rows * gbuf[k][0:1]).astype(BF)

    far, near = 1 - zh, zh
    for side, half in ((0, far), (1, near)):
        pacc[side] = dot(scaled(c, half), pbuf[c])
    s_t.wait_recv()
    s_p.wait_recv()
    s_g.wait_recv()

    def partial(side, half):
        total = pacc[side] + dot(scaled(sib, half), pbuf[sib])
        part[side] = total.astype(BF).reshape(4, 64, 1024)

    partial(0, far)
    s_f = []
    for k in range(2):
        rows = slice(32 * k, 32 * k + 32)
        s_f.append([
            send(part.at[0, x2, rows], fx.at[2, rows], at(dx=2)),
            send(part.at[0, x1, rows], fx.at[0, rows], at(dx=1)),
            send(part.at[0, x3, rows], fx.at[1, rows], at(dx=-1)),
        ])
    ones = jnp.ones((8, 256), BF)
    squares = jnp.zeros((8, 512), F32)
    for k in range(2):
        rows = tbuf[k].reshape(512, 256).astype(F32)
        sq = rows * rows
        hi = sq.astype(BF)
        lo = (sq - hi.astype(F32)).astype(BF)
        squares += lax.dot_general(ones, hi, NT, preferred_element_type=F32)
        squares += lax.dot_general(ones, lo, NT, preferred_element_type=F32)
    for k in range(4):
        ssp[k] = squares[:, 128 * k : 128 * (k + 1)]
    s_ss = [
        send(ssp.at[x1], ssr.at[0], at(dx=1)),
        send(ssp.at[x3], ssr.at[1], at(dx=-1)),
        send(ssp.at[x2], ssr.at[2], at(dx=2)),
    ]

    partial(1, near)

    def first_hop():
        return (
            send(part.at[1, x2, 0:32], rel.at[0], at(dx=1)),
            send(part.at[1, x2, 32:64], rel.at[1], at(dx=-1)),
            send(part.at[1, x1, 32:64], rx.at[0, 32:64], at(dx=1)),
            send(part.at[1, x3, 0:32], rx.at[1, 0:32], at(dx=-1)),
        )

    def second_hop():
        s_x[0].wait_recv()
        stg[0] = (part[1, x1, 0:32].astype(F32) + rel[0].astype(F32)).astype(BF)
        a = send(stg.at[0], rx.at[0, 0:32], at(dx=1))
        s_x[1].wait_recv()
        stg[1] = (part[1, x3, 32:64].astype(F32) + rel[1].astype(F32)).astype(BF)
        b = send(stg.at[1], rx.at[1, 32:64], at(dx=-1))
        return a, b

    def spread_near(place):
        up[place] = send_w(every, at_place(y, place), dy=1)
        down[place] = send_w(every, at_place(y, place), dy=-1)

    s_yn, s_sn = [], []

    def relay_near(place):
        up[place].wait_recv()
        s_yn.append(send_w(slice(0, 2), at_place(y3, place), dy=1))
        down[place].wait_recv()
        s_yn.append(send_w(slice(2, 4), at_place(y1, place), dy=-1))

    def share_near(yy):
        for first_place, count in ((0, 4), (5, 3)):
            rows = pl.ds(pl.multiple_of(yy * 256 + 32 * first_place, 32), 32 * count)
            s_sn.append(send_w(every, rows, core=sib))

    s_wy, s_ws = {}, {}

    def spread_far(r):
        s_wy[r] = [send_w(ring[r], far_rows(y), dy=1), send_w(ring[r], far_rows(y), dy=-1)]
        s_ws[r] = [send_w(ring[r], far_rows(y), core=sib)]

    def relay_far(r):
        s_wy[r][0].wait_recv()
        s_wy[r].append(send_w(ring[r], far_half(y3, 0), dy=1))
        s_ws[r].append(send_w(ring[r], far_rows(y3), core=sib))
        s_wy[r][1].wait_recv()
        s_wy[r].append(send_w(ring[r], far_half(y1, 1), dy=-1))
        s_ws[r].append(send_w(ring[r], far_rows(y1), core=sib))

    def finish_far(r):
        for copy in s_wy[r][2:]:
            copy.wait_recv()
        s_ws[r].append(send_w(ring[r], far_rows(y2), core=sib))

    def across(k):
        rows = slice(32 * k, 32 * k + 32)
        for copy in s_f[k]:
            copy.wait_recv()
        total = part[0, x, rows].astype(F32) + fx[0, rows].astype(F32)
        total = total + fx[1, rows].astype(F32) + fx[2, rows].astype(F32)
        zs[rows] = total.astype(BF)
        return send(zs.at[rows], zf.at[rows], at(dz=8))

    def pass_on(up_place, down_place):
        for k in range(2):
            for place, dz in ((up_place, 1), (down_place, -1)):
                from_z[place, k].wait_recv()
                from_z[(place - dz) % 8, k] = along_z(place, dz, halves[k])

    pass_on(7, 1)
    spread_near(7)
    spread_near(1)
    relay_near(0)
    f3, f1 = x3 * 4 + zh * 2 + c, x1 * 4 + zh * 2 + c
    s_tp.wait_recv()
    s_tm.wait_recv()
    s_tx = [
        send(tab.at[f3, 0:32], tab.at[f3, 0:32], at(dx=1)),
        send(tab.at[f1, 32:64], tab.at[f1, 32:64], at(dx=-1)),
        send(tab.at[f3], tab.at[f3], at(core=sib)),
        send(tab.at[f1], tab.at[f1], at(core=sib)),
    ]
    fz = x * 4 + (1 - zh) * 2 + c
    s_tz.wait_recv()
    s_ty = [send(tab.at[fz, quarter], tab.at[fz, quarter], at(dy=k)) for k in (1, -1, 2)]
    pass_on(6, 2)
    spread_near(6)
    s_z = [across(0)]
    for copy in s_ss:
        copy.wait_recv()
    ssx[...] = ssp[x] + ssr[0] + ssr[1] + ssr[2]
    s_ssz = send(ssx, ssz, at(dz=8))
    s_z.append(across(1))
    far_z[0].wait_recv()
    s_wx = [send_w(x, far_rows(y), dx=k) for k in (1, -1, 2)]
    s_x = first_hop()
    for copy in s_ty:
        copy.wait_recv()
    s_uz = [send(tab.at[fz], tab.at[fz], at(dx=k)) for k in (2, 1, -1)]
    s_us = [send(tab.at[fz], tab.at[fz], at(core=sib))]
    relay_near(7)
    spread_near(2)
    relay_near(1)

    ids = codes[...]
    row = lax.broadcasted_iota(jnp.int32, (512, 64), 0)
    col = lax.broadcasted_iota(jnp.int32, (512, 64), 1)
    spread = (row // 8 == col).astype(BF)
    high = (ids // 32).astype(F32).astype(BF)
    low = lax.rem(ids, 32).astype(F32).astype(BF)
    high = lax.dot_general(spread, high, NT, preferred_element_type=F32)
    low = lax.dot_general(spread, low, NT, preferred_element_type=F32)
    row8 = lax.broadcasted_iota(jnp.int32, (512, 8), 0)
    col8 = lax.broadcasted_iota(jnp.int32, (512, 8), 1)
    picked = jnp.where(lax.rem(row8, 8) == col8, high * 32.0 + low, 0.0)
    id_col = jnp.sum(picked, axis=1, keepdims=True).astype(jnp.int32)

    hops = second_hop()
    f2 = x2 * 4 + zh * 2 + c
    s_tx[0].wait_recv()
    s_tx[1].wait_recv()
    s_tx.append(send(tab.at[f2], tab.at[f2], at(core=sib)))
    for place in (5, 3):
        for k in range(2):
            from_z[place, k].wait_recv()
        spread_near(place)
    relay_near(6)
    share_near(y)
    spread_far(0)
    for r in (1, 2, 3):
        s_wx[r - 1].wait_recv()
        spread_far(r)
    for copy, xx in zip(s_uz, (x2, x3, x1)):
        copy.wait_recv()
        ref = tab.at[xx * 4 + (1 - zh) * 2 + c]
        s_us.append(send(ref, ref, at(core=sib)))
    relay_near(2)
    l_tab.wait()
    for copy in [s_ts] + s_tx[2:] + s_us:
        copy.wait_recv()

    lanes = lax.broadcasted_iota(jnp.int32, (128, 1024), 1)
    whole_table = tab[...].reshape(1024, 1024)
    for t in range(4):
        onehot = (lanes == id_col[128 * t : 128 * (t + 1)]).astype(F32).astype(BF)
        emb[128 * t : 128 * (t + 1)] = dot(onehot, whole_table).astype(BF)

    relay_near(5)
    relay_near(3)
    share_near(y1)
    share_near(y3)

    for copy in s_x[2:] + hops:
        copy.wait_recv()
    total = part[1, x].astype(F32) + rx[0].astype(F32) + rx[1].astype(F32)
    s_ssz.wait_recv()
    sums = ssx[...] + ssz[...]
    lane = lax.broadcasted_iota(jnp.int32, (64, 128), 1)
    sub = lax.broadcasted_iota(jnp.int32, (64, 128), 0)
    sum_col = jnp.sum(
        jnp.where(lane == sub + 64 * zh, sums[0:1], 0.0), axis=1, keepdims=True
    )
    inv_rms = lax.rsqrt(sum_col * (1.0 / 4096.0) + 1e-05)
    for copy in s_z:
        copy.wait_recv()
    context = ((total + zf[...].astype(F32)) * inv_rms).astype(BF).astype(F32)
    depth_gain = dgain[...].astype(F32).reshape(1, 1024)
    turn = lax.rem(256 - 32 * zl, 256)
    for t in range(4):
        rows = slice(128 * t, 128 * (t + 1))
        wide = jnp.broadcast_to(context[16 * t : 16 * (t + 1)][:, None, :], (16, 8, 1024))
        value = wide.reshape(128, 1024) + emb[rows].astype(F32)
        inv = lax.rsqrt(jnp.mean(value * value, axis=-1, keepdims=True) + 1e-05)
        stream[rows] = value
        value = value * inv * depth_gain
        for k in range(4):
            part_k = pltpu.roll(value[:, 256 * k : 256 * (k + 1)], turn, 1)
            normed[rows, 256 * k : 256 * (k + 1)] = part_k.astype(BF)
    relay_far(0)
    relay_far(1)
    relay_far(2)
    relay_far(3)

    def columns(yy):
        return pl.ds(pl.multiple_of(yy * 256, 256), 256)

    def product(r, rows, yy):
        return dot(normed[rows, columns(yy)], wb[ring[r], columns(yy)])

    for copy in s_sn:
        copy.wait_recv()
    for r in range(4):
        for copy in s_ws[r]:
            copy.wait_recv()
        for t in range(2):
            rows = slice(256 * t, 256 * (t + 1))
            early[r, rows] = product(r, rows, y) + product(r, rows, y1) + product(r, rows, y3)
        if r == 0:
            for copy in s_yn:
                copy.wait_recv()
            s_so = len(s_sn)
            share_near(y2)
    last = []
    for r in range(4):
        finish_far(r)
        last.append(s_ws[r][-1])

    first = lax.broadcasted_iota(jnp.int32, (128, 128), 1) < 64
    frame_of_lane = lax.broadcasted_iota(jnp.int32, (8, 128), 1) // 8
    position = lax.broadcasted_iota(jnp.int32, (128, 128), 0)
    query = lax.broadcasted_iota(jnp.int32, (128, 128), 1)
    allowed = lax.rem(position, 8) <= lax.rem(query, 8)
    def by_head(a):
        a = a.astype(F32)
        return jnp.concatenate(
            [jnp.where(first, a, 0.0).astype(BF), jnp.where(first, 0.0, a).astype(BF)], axis=0
        )

    def attend(r):
        for t in range(2):
            rows = slice(256 * t, 256 * (t + 1))
            qkv[rows] = (early[r, rows] + product(r, rows, y2)).astype(BF)
        for t in range(4):
            rows = slice(128 * t, 128 * (t + 1))
            for b in range(2):
                q = qkv[rows, 384 * b : 384 * b + 128]
                k = by_head(qkv[rows, 384 * b + 128 : 384 * b + 256])
                scores = lax.dot_general(k, q, NT, preferred_element_type=F32)
                for h in range(2):
                    own = scores[128 * h : 128 * h + 8]
                    for f in range(1, 16):
                        own = jnp.where(
                            frame_of_lane == f, scores[128 * h + 8 * f : 128 * h + 8 * f + 8], own
                        )
                    unit = t * 4 + b * 2 + h
                    comp[8 * unit : 8 * unit + 8] = own
        scores = jnp.where(allowed, comp[...] * 0.125, -1e30).reshape(16, 8, 128)
        e = jnp.exp(scores - jnp.max(scores, axis=1, keepdims=True))
        weights = (e / jnp.sum(e, axis=1, keepdims=True)).reshape(128, 128)
        for t in range(4):
            rows = slice(128 * t, 128 * (t + 1))
            for b in range(2):
                wide = []
                for unit in (t * 4 + b * 2, t * 4 + b * 2 + 1):
                    own = weights[8 * unit : 8 * unit + 8]
                    wide += [jnp.where(frame_of_lane == f, own, 0.0) for f in range(16)]
                wide = jnp.concatenate(wide, axis=0).astype(BF)
                v = by_head(qkv[rows, 384 * b + 256 : 384 * b + 384])
                mixed[rows, 256 * r + 128 * b : 256 * r + 128 * b + 128] = lax.dot_general(
                    wide, v, TN, preferred_element_type=F32
                ).astype(BF)

    for copy in l_out:
        copy.wait()
    for copy in s_sn[s_so:]:
        copy.wait_recv()
    for r in range(4):
        last[r].wait_recv()
        if r == 3:
            for t in range(4):
                rows = slice(128 * t, 128 * (t + 1))
                stream[rows] = stream[rows] + dot(mixed[rows, :768], doutb[:768])
        attend(r)
    stores = []
    for t in range(4):
        rows = slice(128 * t, 128 * (t + 1))
        outb[rows] = (stream[rows] + dot(mixed[rows, 768:], doutb[768:])).astype(BF)
        stores.append(load(outb.at[rows], out.at[rows]))
    for copy in stores:
        copy.wait()

    for copy in started:
        copy.wait_send()


def per_device(
    temporal_out, norm_gain, input_proj, code_table, depth_gain, depth_proj, depth_out, code_ids
):
    vmem = pl.BlockSpec(memory_space=pltpu.VMEM)
    hbm = pl.BlockSpec(memory_space=pl.ANY)
    scratch = [
        ((2, 4, 2, 64, 256), BF),
        ((2, 256, 1024), BF),
        ((2, 8, 256), F32),
        ((2, 256, 1024), F32),
        ((2, 4, 64, 1024), BF),
        ((2, 32, 1024), BF),
        ((2, 64, 1024), BF),
        ((2, 32, 1024), BF),
        ((3, 64, 1024), BF),
        ((64, 1024), BF),
        ((64, 1024), BF),
        ((4, 8, 128), F32),
        ((3, 8, 128), F32),
        ((8, 128), F32),
        ((8, 128), F32),
        ((16, 64, 1024), BF),
        ((512, 1024), BF),
        ((512, 1024), BF),
        ((512, 1024), F32),
        ((4, 1024, 768), BF),
        ((4, 512, 768), F32),
        ((512, 768), BF),
        ((128, 128), F32),
        ((512, 1024), BF),
        ((1024, 1024), BF),
        ((512, 1024), BF),
    ]
    operands = (
        temporal_out.reshape(4, 2, 2, 64, 256),
        norm_gain,
        input_proj,
        code_table,
        depth_gain,
        depth_proj,
        depth_out,
        code_ids.reshape(64, 8).T,
    )
    result = pl.pallas_call(
        kernel,
        out_shape=jax.ShapeDtypeStruct((512, 1024), BF),
        in_specs=[hbm, vmem, hbm, hbm, vmem, hbm, hbm, vmem],
        out_specs=hbm,
        scratch_shapes=[pltpu.VMEM(shape, dtype) for shape, dtype in scratch]
        + [
            pltpu.SemaphoreType.DMA((N_REMOTE,)),
            pltpu.SemaphoreType.DMA((N_REMOTE,)),
            pltpu.SemaphoreType.DMA((32,)),
        ],
        compiler_params=pltpu.CompilerParams(
            collective_id=0, has_side_effects=True, vmem_limit_bytes=44 * 1024 * 1024
        ),
        cost_estimate=pl.CostEstimate(
            flops=6_500_000_000, bytes_accessed=6_000_000, transcendentals=2_000_000
        ),
    )(*(pltpu.with_memory_space_constraint(a, pltpu.HBM) for a in operands))
    return result.reshape(1, 1, 64, 8, 1024)


def solution(mesh):
    placed = (
        P("frame", "fsdp"),
        P("fsdp"),
        P("fsdp", None),
        P("fsdp", None),
        P(),
        P("frame", None),
        P(),
        P("frame", "fsdp", None, None),
    )
    return jax.shard_map(
        per_device,
        mesh=mesh,
        in_specs=placed,
        out_specs=P("frame", "fsdp", None, None, None),
        check_vma=False,
    )
```

```python
import functools

import jax
import jax.numpy as jnp
from jax import lax
from jax.experimental import pallas as pl
from jax.experimental.pallas import tpu as pltpu
from jax.sharding import PartitionSpec as P

BF = jnp.bfloat16
F32 = jnp.float32
MESH = pl.DeviceIdType.MESH
NT = (((1,), (1,)), ((), ()))
TN = (((0,), (0,)), ((), ()))
N_REMOTE = 128


def dot(a, b):
    return jnp.dot(a, b, preferred_element_type=F32)


def kernel(
    temporal, gain, proj, table, dgain, dproj, dout, codes,
    out,
    tbuf, pbuf, gbuf, pacc, part, rel, rx, stg, fx, zs, zf,
    ssp, ssr, ssx, ssz,
    tab, emb, normed, stream,
    wb, early, qkv, comp, mixed, doutb, outb,
    ssem, rsem, lsem,
):
    fs = lax.axis_index("fsdp")
    fr = lax.axis_index("frame")
    x, zh, c = fs // 4, lax.rem(fs // 2, 2), lax.rem(fs, 2)
    y, zl = fr // 8, lax.rem(fr, 8)
    z = zh * 8 + zl
    sib = 1 - c

    def at(dx=0, dy=0, dz=0, core=None):
        tx, ty, tz = lax.rem(x + dx + 4, 4), lax.rem(y + dy + 4, 4), lax.rem(z + dz + 16, 16)
        tc = c if core is None else core
        return (tx * 4 + (tz // 8) * 2 + tc, ty * 8 + lax.rem(tz, 8))

    x1, x2, x3 = lax.rem(x + 1, 4), lax.rem(x + 2, 4), lax.rem(x + 3, 4)
    y1, y2, y3 = lax.rem(y + 1, 4), lax.rem(y + 2, 4), lax.rem(y + 3, 4)

    started = []

    def send(src, dst, dev):
        index = len(started)
        copy = pltpu.make_async_remote_copy(
            src_ref=src, dst_ref=dst, send_sem=ssem.at[index], recv_sem=rsem.at[index],
            device_id=dev, device_id_type=MESH,
        )
        copy.start()
        started.append(copy)
        return copy

    locals_ = []

    def load(src, dst):
        copy = pltpu.make_async_copy(src, dst, lsem.at[len(locals_)])
        copy.start()
        locals_.append(copy)
        return copy

    mine = pl.ds(pl.multiple_of(c * 384, 128), 384)
    ring = [lax.rem(x + k, 4) for k in (0, 3, 1, 2)]

    def at_place(yy, place):
        return pl.ds(pl.multiple_of(yy * 256 + 32 * place, 32), 32)

    def far_rows(yy):
        return at_place(yy, 4)

    def far_half(yy, k):
        return pl.ds(pl.multiple_of(yy * 256 + 128 + 16 * k, 16), 16)

    l_w = [
        load(
            dproj.at[:, pl.ds(pl.multiple_of(k * 1024 + (2 * xx + c) * 128, 128), 128)],
            wb.at[xx, at_place(y, 0), pl.ds(pl.multiple_of(c * 384 + k * 128, 128), 128)],
        )
        for xx in range(4)
        for k in range(3)
    ]
    l_t = load(temporal.at[:, :, c], tbuf.at[c])
    l_p = load(proj, pbuf.at[c])
    l_tab = load(table, tab.at[fs])
    l_out = [
        load(dout.at[pl.ds(pl.multiple_of(ring[r] * 256, 256), 256)], doutb.at[256 * r : 256 * r + 256])
        for r in range(4)
    ]
    gbuf[c] = jnp.broadcast_to(gain[...].astype(F32).reshape(1, 256), (8, 256))

    partners = [at(core=sib)]
    partners += [at(dx=k) for k in (1, -1, 2)] + [at(dy=k) for k in (1, -1, 2)]
    partners += [at(dz=k) for k in (1, -1, 4, -4, 8)]
    barrier = pltpu.get_barrier_semaphore()
    partners.append((x * 4 + (1 - zh) * 2 + c, y * 8 + 7 - zl))
    for partner in partners:
        pl.semaphore_signal(barrier, inc=1, device_id=partner, device_id_type=MESH)
    pl.semaphore_wait(barrier, len(partners))

    quarter = pl.ds(pl.multiple_of(y * 16, 16), 16)
    mirror = (x * 4 + (1 - zh) * 2 + c, y * 8 + 7 - zl)
    s_tz = send(table.at[quarter], tab.at[fs, quarter], mirror)
    for copy in l_w:
        copy.wait()

    def send_w(xx, rows, **to):
        ref = wb.at[xx, rows, mine]
        return send(ref, ref, at(**to))

    every = slice(0, 4)

    def along_z(place, dz, pieces=slice(0, 4)):
        return send(
            wb.at[pieces, at_place(y, place), mine],
            wb.at[pieces, at_place(y, (place - dz) % 8), mine],
            at(dz=dz),
        )

    halves = (slice(0, 2), slice(2, 4))
    from_z = {}
    for k in range(2):
        for place, dz in ((7, 1), (1, -1)):
            from_z[place, k] = along_z(0, dz, halves[k])
    up = {0: send_w(every, at_place(y, 0), dy=1)}
    down = {0: send_w(every, at_place(y, 0), dy=-1)}
    far_z = [
        send(wb.at[x, at_place(y, 0), mine], wb.at[x, at_place(y, -k % 8), mine], at(dz=k))
        for k in (4,)
    ]
    s_t = send(temporal.at[:, :, sib], tbuf.at[c], at(core=sib))
    s_p = send(proj, pbuf.at[c], at(core=sib))
    s_g = send(gbuf.at[c], gbuf.at[c], at(core=sib))
    s_tp = send(table, tab.at[fs], at(dx=1))
    s_tm = send(table, tab.at[fs], at(dx=-1))
    s_ts = send(table, tab.at[fs], at(core=sib))

    l_t.wait()
    l_p.wait()

    def scaled(k, half):
        rows = tbuf[k, :, half].reshape(256, 256).astype(F32)
        return (rows * gbuf[k][0:1]).astype(BF)

    far, near = 1 - zh, zh
    for side, half in ((0, far), (1, near)):
        pacc[side] = dot(scaled(c, half), pbuf[c])
    s_t.wait_recv()
    s_p.wait_recv()
    s_g.wait_recv()

    def partial(side, half):
        total = pacc[side] + dot(scaled(sib, half), pbuf[sib])
        part[side] = total.astype(BF).reshape(4, 64, 1024)

    partial(0, far)
    s_f = []
    for k in range(2):
        rows = slice(32 * k, 32 * k + 32)
        s_f.append([
            send(part.at[0, x2, rows], fx.at[2, rows], at(dx=2)),
            send(part.at[0, x1, rows], fx.at[0, rows], at(dx=1)),
            send(part.at[0, x3, rows], fx.at[1, rows], at(dx=-1)),
        ])
    ones = jnp.ones((8, 256), BF)
    squares = jnp.zeros((8, 512), F32)
    for k in range(2):
        rows = tbuf[k].reshape(512, 256).astype(F32)
        sq = rows * rows
        hi = sq.astype(BF)
        lo = (sq - hi.astype(F32)).astype(BF)
        squares += lax.dot_general(ones, hi, NT, preferred_element_type=F32)
        squares += lax.dot_general(ones, lo, NT, preferred_element_type=F32)
    for k in range(4):
        ssp[k] = squares[:, 128 * k : 128 * (k + 1)]
    s_ss = [
        send(ssp.at[x1], ssr.at[0], at(dx=1)),
        send(ssp.at[x3], ssr.at[1], at(dx=-1)),
        send(ssp.at[x2], ssr.at[2], at(dx=2)),
    ]

    partial(1, near)

    def first_hop():
        return (
            send(part.at[1, x2, 0:32], rel.at[0], at(dx=1)),
            send(part.at[1, x2, 32:64], rel.at[1], at(dx=-1)),
            send(part.at[1, x1, 32:64], rx.at[0, 32:64], at(dx=1)),
            send(part.at[1, x3, 0:32], rx.at[1, 0:32], at(dx=-1)),
        )

    def second_hop():
        s_x[0].wait_recv()
        stg[0] = (part[1, x1, 0:32].astype(F32) + rel[0].astype(F32)).astype(BF)
        a = send(stg.at[0], rx.at[0, 0:32], at(dx=1))
        s_x[1].wait_recv()
        stg[1] = (part[1, x3, 32:64].astype(F32) + rel[1].astype(F32)).astype(BF)
        b = send(stg.at[1], rx.at[1, 32:64], at(dx=-1))
        return a, b

    def spread_near(place):
        up[place] = send_w(every, at_place(y, place), dy=1)
        down[place] = send_w(every, at_place(y, place), dy=-1)

    s_yn, s_sn = [], []

    def relay_near(place):
        up[place].wait_recv()
        s_yn.append(send_w(slice(0, 2), at_place(y3, place), dy=1))
        down[place].wait_recv()
        s_yn.append(send_w(slice(2, 4), at_place(y1, place), dy=-1))

    def share_near(yy):
        for first_place, count in ((0, 4), (5, 3)):
            rows = pl.ds(pl.multiple_of(yy * 256 + 32 * first_place, 32), 32 * count)
            s_sn.append(send_w(every, rows, core=sib))

    s_wy, s_ws = {}, {}

    def spread_far(r):
        s_wy[r] = [send_w(ring[r], far_rows(y), dy=1), send_w(ring[r], far_rows(y), dy=-1)]
        s_ws[r] = [send_w(ring[r], far_rows(y), core=sib)]

    def relay_far(r):
        s_wy[r][0].wait_recv()
        s_wy[r].append(send_w(ring[r], far_half(y3, 0), dy=1))
        s_ws[r].append(send_w(ring[r], far_rows(y3), core=sib))
        s_wy[r][1].wait_recv()
        s_wy[r].append(send_w(ring[r], far_half(y1, 1), dy=-1))
        s_ws[r].append(send_w(ring[r], far_rows(y1), core=sib))

    def finish_far(r):
        for copy in s_wy[r][2:]:
            copy.wait_recv()
        s_ws[r].append(send_w(ring[r], far_rows(y2), core=sib))

    def across(k):
        rows = slice(32 * k, 32 * k + 32)
        for copy in s_f[k]:
            copy.wait_recv()
        total = part[0, x, rows].astype(F32) + fx[0, rows].astype(F32)
        total = total + fx[1, rows].astype(F32) + fx[2, rows].astype(F32)
        zs[rows] = total.astype(BF)
        return send(zs.at[rows], zf.at[rows], at(dz=8))

    def pass_on(up_place, down_place):
        for k in range(2):
            for place, dz in ((up_place, 1), (down_place, -1)):
                from_z[place, k].wait_recv()
                from_z[(place - dz) % 8, k] = along_z(place, dz, halves[k])

    pass_on(7, 1)
    spread_near(7)
    spread_near(1)
    relay_near(0)
    f3, f1 = x3 * 4 + zh * 2 + c, x1 * 4 + zh * 2 + c
    s_tp.wait_recv()
    s_tm.wait_recv()
    s_tx = [
        send(tab.at[f3, 0:32], tab.at[f3, 0:32], at(dx=1)),
        send(tab.at[f1, 32:64], tab.at[f1, 32:64], at(dx=-1)),
        send(tab.at[f3], tab.at[f3], at(core=sib)),
        send(tab.at[f1], tab.at[f1], at(core=sib)),
    ]
    fz = x * 4 + (1 - zh) * 2 + c
    s_tz.wait_recv()
    s_ty = [send(tab.at[fz, quarter], tab.at[fz, quarter], at(dy=k)) for k in (1, -1, 2)]
    pass_on(6, 2)
    spread_near(6)
    s_z = [across(0)]
    for copy in s_ss:
        copy.wait_recv()
    ssx[...] = ssp[x] + ssr[0] + ssr[1] + ssr[2]
    s_ssz = send(ssx, ssz, at(dz=8))
    s_z.append(across(1))
    far_z[0].wait_recv()
    s_wx = [send_w(x, far_rows(y), dx=k) for k in (1, -1, 2)]
    s_x = first_hop()
    for copy in s_ty:
        copy.wait_recv()
    s_uz = [send(tab.at[fz], tab.at[fz], at(dx=k)) for k in (2, 1, -1)]
    s_us = [send(tab.at[fz], tab.at[fz], at(core=sib))]
    relay_near(7)
    spread_near(2)
    relay_near(1)

    ids = codes[...]
    row = lax.broadcasted_iota(jnp.int32, (512, 64), 0)
    col = lax.broadcasted_iota(jnp.int32, (512, 64), 1)
    spread = (row // 8 == col).astype(BF)
    high = (ids // 32).astype(F32).astype(BF)
    low = lax.rem(ids, 32).astype(F32).astype(BF)
    high = lax.dot_general(spread, high, NT, preferred_element_type=F32)
    low = lax.dot_general(spread, low, NT, preferred_element_type=F32)
    row8 = lax.broadcasted_iota(jnp.int32, (512, 8), 0)
    col8 = lax.broadcasted_iota(jnp.int32, (512, 8), 1)
    picked = jnp.where(lax.rem(row8, 8) == col8, high * 32.0 + low, 0.0)
    id_col = jnp.sum(picked, axis=1, keepdims=True).astype(jnp.int32)

    hops = second_hop()
    f2 = x2 * 4 + zh * 2 + c
    s_tx[0].wait_recv()
    s_tx[1].wait_recv()
    s_tx.append(send(tab.at[f2], tab.at[f2], at(core=sib)))
    for place in (5, 3):
        for k in range(2):
            from_z[place, k].wait_recv()
        spread_near(place)
    relay_near(6)
    share_near(y)
    spread_far(0)
    for r in (1, 2, 3):
        s_wx[r - 1].wait_recv()
        spread_far(r)
    for copy, xx in zip(s_uz, (x2, x3, x1)):
        copy.wait_recv()
        ref = tab.at[xx * 4 + (1 - zh) * 2 + c]
        s_us.append(send(ref, ref, at(core=sib)))
    relay_near(2)
    relay_near(5)
    l_tab.wait()
    for copy in [s_ts] + s_tx[2:] + s_us:
        copy.wait_recv()

    lanes = lax.broadcasted_iota(jnp.int32, (128, 1024), 1)
    whole_table = tab[...].reshape(1024, 1024)
    for t in range(4):
        onehot = (lanes == id_col[128 * t : 128 * (t + 1)]).astype(F32).astype(BF)
        emb[128 * t : 128 * (t + 1)] = dot(onehot, whole_table).astype(BF)

    relay_near(3)
    share_near(y1)
    share_near(y3)

    for copy in s_x[2:] + hops:
        copy.wait_recv()
    total = part[1, x].astype(F32) + rx[0].astype(F32) + rx[1].astype(F32)
    s_ssz.wait_recv()
    sums = ssx[...] + ssz[...]
    lane = lax.broadcasted_iota(jnp.int32, (64, 128), 1)
    sub = lax.broadcasted_iota(jnp.int32, (64, 128), 0)
    sum_col = jnp.sum(
        jnp.where(lane == sub + 64 * zh, sums[0:1], 0.0), axis=1, keepdims=True
    )
    inv_rms = lax.rsqrt(sum_col * (1.0 / 4096.0) + 1e-05)
    for copy in s_z:
        copy.wait_recv()
    context = ((total + zf[...].astype(F32)) * inv_rms).astype(BF).astype(F32)
    depth_gain = dgain[...].astype(F32).reshape(1, 1024)
    turn = lax.rem(256 - 32 * zl, 256)
    for t in range(4):
        rows = slice(128 * t, 128 * (t + 1))
        wide = jnp.broadcast_to(context[16 * t : 16 * (t + 1)][:, None, :], (16, 8, 1024))
        value = wide.reshape(128, 1024) + emb[rows].astype(F32)
        inv = lax.rsqrt(jnp.mean(value * value, axis=-1, keepdims=True) + 1e-05)
        stream[rows] = value
        value = value * inv * depth_gain
        for k in range(4):
            part_k = pltpu.roll(value[:, 256 * k : 256 * (k + 1)], turn, 1)
            normed[rows, 256 * k : 256 * (k + 1)] = part_k.astype(BF)
    relay_far(0)
    relay_far(1)
    relay_far(2)
    relay_far(3)

    def columns(yy):
        return pl.ds(pl.multiple_of(yy * 256, 256), 256)

    def product(r, rows, yy):
        return dot(normed[rows, columns(yy)], wb[ring[r], columns(yy)])

    for copy in s_sn:
        copy.wait_recv()
    for r in range(4):
        for copy in s_ws[r]:
            copy.wait_recv()
        for t in range(2):
            rows = slice(256 * t, 256 * (t + 1))
            early[r, rows] = product(r, rows, y) + product(r, rows, y1) + product(r, rows, y3)
        if r == 0:
            for copy in s_yn:
                copy.wait_recv()
            s_so = len(s_sn)
            share_near(y2)
    last = []
    for r in range(4):
        finish_far(r)
        last.append(s_ws[r][-1])

    first = lax.broadcasted_iota(jnp.int32, (128, 128), 1) < 64
    frame_of_lane = lax.broadcasted_iota(jnp.int32, (8, 128), 1) // 8
    position = lax.broadcasted_iota(jnp.int32, (128, 128), 0)
    query = lax.broadcasted_iota(jnp.int32, (128, 128), 1)
    allowed = lax.rem(position, 8) <= lax.rem(query, 8)
    def by_head(a):
        a = a.astype(F32)
        return jnp.concatenate(
            [jnp.where(first, a, 0.0).astype(BF), jnp.where(first, 0.0, a).astype(BF)], axis=0
        )

    def attend(r):
        for t in range(2):
            rows = slice(256 * t, 256 * (t + 1))
            qkv[rows] = (early[r, rows] + product(r, rows, y2)).astype(BF)
        for t in range(4):
            rows = slice(128 * t, 128 * (t + 1))
            for b in range(2):
                q = qkv[rows, 384 * b : 384 * b + 128]
                k = by_head(qkv[rows, 384 * b + 128 : 384 * b + 256])
                scores = lax.dot_general(k, q, NT, preferred_element_type=F32)
                for h in range(2):
                    own = scores[128 * h : 128 * h + 8]
                    for f in range(1, 16):
                        own = jnp.where(
                            frame_of_lane == f, scores[128 * h + 8 * f : 128 * h + 8 * f + 8], own
                        )
                    unit = t * 4 + b * 2 + h
                    comp[8 * unit : 8 * unit + 8] = own
        scores = jnp.where(allowed, comp[...] * 0.125, -1e30).reshape(16, 8, 128)
        e = jnp.exp(scores - jnp.max(scores, axis=1, keepdims=True))
        weights = (e / jnp.sum(e, axis=1, keepdims=True)).reshape(128, 128)
        for t in range(4):
            rows = slice(128 * t, 128 * (t + 1))
            for b in range(2):
                wide = []
                for unit in (t * 4 + b * 2, t * 4 + b * 2 + 1):
                    own = weights[8 * unit : 8 * unit + 8]
                    wide += [jnp.where(frame_of_lane == f, own, 0.0) for f in range(16)]
                wide = jnp.concatenate(wide, axis=0).astype(BF)
                v = by_head(qkv[rows, 384 * b + 256 : 384 * b + 384])
                mixed[rows, 256 * r + 128 * b : 256 * r + 128 * b + 128] = lax.dot_general(
                    wide, v, TN, preferred_element_type=F32
                ).astype(BF)

    for copy in l_out:
        copy.wait()
    for copy in s_sn[s_so:]:
        copy.wait_recv()
    for r in range(4):
        last[r].wait_recv()
        if r == 3:
            for t in range(4):
                rows = slice(128 * t, 128 * (t + 1))
                stream[rows] = stream[rows] + dot(mixed[rows, :768], doutb[:768])
        attend(r)
    stores = []
    for t in range(4):
        rows = slice(128 * t, 128 * (t + 1))
        outb[rows] = (stream[rows] + dot(mixed[rows, 768:], doutb[768:])).astype(BF)
        stores.append(load(outb.at[rows], out.at[rows]))
    for copy in stores:
        copy.wait()

    for copy in started:
        copy.wait_send()


def per_device(
    temporal_out, norm_gain, input_proj, code_table, depth_gain, depth_proj, depth_out, code_ids
):
    vmem = pl.BlockSpec(memory_space=pltpu.VMEM)
    hbm = pl.BlockSpec(memory_space=pl.ANY)
    scratch = [
        ((2, 4, 2, 64, 256), BF),
        ((2, 256, 1024), BF),
        ((2, 8, 256), F32),
        ((2, 256, 1024), F32),
        ((2, 4, 64, 1024), BF),
        ((2, 32, 1024), BF),
        ((2, 64, 1024), BF),
        ((2, 32, 1024), BF),
        ((3, 64, 1024), BF),
        ((64, 1024), BF),
        ((64, 1024), BF),
        ((4, 8, 128), F32),
        ((3, 8, 128), F32),
        ((8, 128), F32),
        ((8, 128), F32),
        ((16, 64, 1024), BF),
        ((512, 1024), BF),
        ((512, 1024), BF),
        ((512, 1024), F32),
        ((4, 1024, 768), BF),
        ((4, 512, 768), F32),
        ((512, 768), BF),
        ((128, 128), F32),
        ((512, 1024), BF),
        ((1024, 1024), BF),
        ((512, 1024), BF),
    ]
    operands = (
        temporal_out.reshape(4, 2, 2, 64, 256),
        norm_gain,
        input_proj,
        code_table,
        depth_gain,
        depth_proj,
        depth_out,
        code_ids.reshape(64, 8).T,
    )
    result = pl.pallas_call(
        kernel,
        out_shape=jax.ShapeDtypeStruct((512, 1024), BF),
        in_specs=[hbm, vmem, hbm, hbm, vmem, hbm, hbm, vmem],
        out_specs=hbm,
        scratch_shapes=[pltpu.VMEM(shape, dtype) for shape, dtype in scratch]
        + [
            pltpu.SemaphoreType.DMA((N_REMOTE,)),
            pltpu.SemaphoreType.DMA((N_REMOTE,)),
            pltpu.SemaphoreType.DMA((32,)),
        ],
        compiler_params=pltpu.CompilerParams(
            collective_id=0, has_side_effects=True, vmem_limit_bytes=44 * 1024 * 1024
        ),
        cost_estimate=pl.CostEstimate(
            flops=6_500_000_000, bytes_accessed=6_000_000, transcendentals=2_000_000
        ),
    )(*(pltpu.with_memory_space_constraint(a, pltpu.HBM) for a in operands))
    return result.reshape(1, 1, 64, 8, 1024)


def solution(mesh):
    placed = (
        P("frame", "fsdp"),
        P("fsdp"),
        P("fsdp", None),
        P("fsdp", None),
        P(),
        P("frame", None),
        P(),
        P("frame", "fsdp", None, None),
    )
    return jax.shard_map(
        per_device,
        mesh=mesh,
        in_specs=placed,
        out_specs=P("frame", "fsdp", None, None, None),
        check_vma=False,
    )
```
